32 devices in a mesh: space: 8 (over z, x), chan: 4 (over y, core).
Axes of the slice: x: 2, y: 2, z: 4, core: 2. Of those that a mesh axis runs over, the one named last changes fastest.
Arguments:
- features: bfloat16 [64, 64, 512], P('space', 'chan'), may hold values from -6 to 6
- weight: bfloat16 [27, 64, 64], P(None, 'chan'), may hold values from -0.15625 to 0.15625
- cotangent: bfloat16 [64, 64, 512], P('space', 'chan'), may hold values from -6 to 6
- neighbours: int32 [64, 27], P('space'), may hold values from -1 to 63, as said below
Outputs:
- output: bfloat16 [64, 64, 512], P('space', 'chan')
- grad_input: bfloat16 [64, 64, 512], P('space', 'chan')
- grad_weight: float32 [27, 64, 64], P(None, 'chan')
The draws below stay inside these ranges and needn't reach their ends.
Inputs may be any that keep to these rules, and one draw needn't show every extreme that they name: `neighbours`: row r lists, for the displacement (i, j, k) in the finite set (-1, 0, 1)^3 at entry 9 (i + 1) + 3 (j + 1) + (k + 1), the slot of the brick at that displacement in bricks, or -1 where the scene has none. Slot s belongs to device s // 8 of space, and a neighbour at first displacement i belongs to the device of index one's own + i. The relation is symmetric: if row r names s at entry m, row s names r at entry 26 - m. A device's occupied bricks fill its first slots, and the last device of space has all 8 slots occupied; an empty slot's row is all -1, no row names an empty slot, and an occupied brick's entry 13 is its own slot.
All inputs are finite; a program needn't handle non-finite values.
Results may differ from the reference program's by a relative error of at most 0.001.
Values may be sent and summed in bfloat16 or wider, within the bound.
No kernel may reach another device: no remote copies, remote signals or barrier semaphores. Data moves between devices by JAX's collectives and lax.ppermute only.
A program may use at most 128 MiB of HBM per device.

```python
import jax
import jax.numpy as jnp
from jax import lax

CHANNELS = 64
B_DEV = 8
CROSS = 8
SLOTS = 64
VOXELS = 32768
N_SPACE = 8


def draw_neighbours(key, part):
    cells = CROSS * CROSS
    key_count, key_full, key_perm = jax.random.split(jax.random.fold_in(key, 11), 3)
    devices = jnp.arange(N_SPACE, dtype=jnp.int32)
    loads = jax.random.randint(key_count, (N_SPACE,), B_DEV // 2, B_DEV + 1)
    busiest = jax.random.randint(key_full, (), 0, N_SPACE)
    loads = jnp.where((devices == busiest) | (devices == N_SPACE - 1), B_DEV, loads)
    orders = jax.vmap(lambda subkey: jax.random.permutation(subkey, cells))(jax.random.split(key_perm, N_SPACE))
    places = jnp.arange(B_DEV, dtype=jnp.int32)
    occupied = places[None, :] < loads[:, None]
    picked = jnp.sort(jnp.where(occupied, orders[:, :B_DEV], cells), axis=1).astype(jnp.int32)
    slot_ids = (devices[:, None] * B_DEV + places[None, :]).astype(jnp.int32)
    device_grid = jnp.broadcast_to(devices[:, None], picked.shape)
    lookup = jnp.full((N_SPACE, cells + 1), -1, jnp.int32)
    lookup = lookup.at[device_grid, picked].set(jnp.where(occupied, slot_ids, -1).astype(jnp.int32))
    lookup = lookup[:, :cells]
    row_y = picked // CROSS
    row_z = picked % CROSS
    entries = []
    for step_x in range(3):
        for step_y in range(3):
            for step_z in range(3):
                near_s = device_grid + step_x - 1
                near_y = row_y + step_y - 1
                near_z = row_z + step_z - 1
                inside = occupied & (near_s >= 0) & (near_s < N_SPACE) & (near_y >= 0) & (near_y < CROSS) & (near_z >= 0) & (near_z < CROSS)
                found = lookup[jnp.clip(near_s, 0, N_SPACE - 1), jnp.clip(near_y, 0, CROSS - 1) * CROSS + jnp.clip(near_z, 0, CROSS - 1)]
                entries.append(jnp.where(inside, found, -1))
    return jnp.stack(entries, axis=-1).reshape(N_SPACE * B_DEV, 27).astype(jnp.int32)


def steps_of(key, dims, cuts, least, largest):
    factor_of = 1.0
    for position, shards_of in cuts:
        draws = jax.random.uniform(jax.random.fold_in(jax.random.fold_in(key, 6), position), (shards_of,), jnp.float32, least / len(cuts), largest / len(cuts))
        factor_of = factor_of * jnp.repeat(jnp.exp(draws), dims[position] // shards_of).reshape((-1,) + (1,) * (len(dims) - 1 - position))
    return factor_of


def normal_values(rng, extent, deviation, most, shards=(), kind=jnp.bfloat16):
    values = jax.random.normal(rng, extent, jnp.float32) * deviation
    if len(shards) > 0:
        values = steps_of(rng, extent, shards, -0.22, 0.18) * values
    return jnp.clip(values, min=-most, max=most).astype(kind)


def setup_inputs(seed: int = 0) -> dict:
    splits = jax.random.split(jax.random.key(seed), 5)
    features = normal_values(splits[0], (SLOTS, CHANNELS, 512), 1.0, 6.0, ((0, 8), (1, 4)))
    weight = normal_values(splits[1], (27, CHANNELS, CHANNELS), (27 * CHANNELS) ** -0.5, 0.15625, ((1, 4),))
    cotangent = normal_values(splits[2], (SLOTS, CHANNELS, 512), 1.0, 6.0, ((0, 8), (1, 4)))
    neighbours = draw_neighbours(jax.random.fold_in(splits[4], 71), 0)
    return {"features": features, "weight": weight, "cotangent": cotangent, "neighbours": neighbours}


def assemble(source, table):
    spans = (slice(7, 8), slice(0, 8), slice(0, 1))
    layers = []
    for step_x in range(3):
        slabs = []
        for step_y in range(3):
            pieces = []
            for step_z in range(3):
                picked = jnp.take(source, table[:, 9 * step_x + 3 * step_y + step_z], axis=0)
                pieces.append(picked[:, :, spans[step_x], spans[step_y], spans[step_z]])
            slabs.append(jnp.concatenate(pieces, axis=4))
        layers.append(jnp.concatenate(slabs, axis=3))
    return jnp.concatenate(layers, axis=2)

def convolve(padded, kernel):
    running = jnp.zeros((padded.shape[0], kernel.shape[1], 8, 8, 8), padded.dtype)
    for step_x in range(3):
        for step_y in range(3):
            for step_z in range(3):
                window = padded[:, :, step_x:step_x + 8, step_y:step_y + 8, step_z:step_z + 8]
                running = running + jnp.einsum('oc,rcxyz->roxyz', kernel[9 * step_x + 3 * step_y + step_z], window)
    return running

def reference(features, weight, cotangent, neighbours):
    slot_total = features.shape[0]
    feat_full = features.astype(jnp.float32).reshape(slot_total, CHANNELS, 8, 8, 8)
    kernel_full = weight.astype(jnp.float32)
    table = jnp.where(neighbours < 0, slot_total, neighbours).astype(jnp.int32)
    blocks = table.reshape(-1, 8 * B_DEV, 27)

    def forward(feat, kernel):
        source = jnp.concatenate([feat, jnp.zeros((1, CHANNELS, 8, 8, 8), feat.dtype)], axis=0)

        def one_block(block_rows):
            return convolve(assemble(source, block_rows), kernel)
        result = lax.map(jax.checkpoint(one_block), blocks)
        return result.reshape(slot_total, CHANNELS, 8, 8, 8)
    output, pullback = jax.vjp(forward, feat_full, kernel_full)
    grad_feat, grad_kernel = pullback(cotangent.astype(jnp.float32).reshape(slot_total, CHANNELS, 8, 8, 8))
    return (output.reshape(slot_total, CHANNELS, 512).astype(jnp.bfloat16), grad_feat.reshape(slot_total, CHANNELS, 512).astype(jnp.bfloat16), grad_kernel * VOXELS ** (-0.5))
```

```python
import functools

import jax
import jax.numpy as jnp
from jax import lax
from jax.experimental import pallas as pl
from jax.experimental.pallas import tpu as pltpu
from jax.sharding import PartitionSpec as P

f32, bf16, i32 = jnp.float32, jnp.bfloat16, jnp.int32
VMEM = pl.BlockSpec(memory_space=pltpu.VMEM)
SMEM = pl.BlockSpec(memory_space=pltpu.SMEM)
PARAMS = pltpu.CompilerParams(vmem_limit_bytes=48 * 1024 * 1024)


def iota(shape, axis):
    return lax.broadcasted_iota(i32, shape, axis)


def call(kernel, out_shape, scratch, *args, specs, flops=0, moved=0):
    return pl.pallas_call(
        kernel,
        out_shape=out_shape,
        in_specs=specs,
        out_specs=jax.tree.map(lambda _: VMEM, out_shape),
        scratch_shapes=scratch,
        compiler_params=PARAMS,
        cost_estimate=pl.CostEstimate(flops=flops, bytes_accessed=moved, transcendentals=0),
    )(*args)


def prepare_kernel(place_ref, feat_ref, cot_ref, weight_ref, sent_ref, first_ref, second_ref):
    rows = feat_ref.shape[0] * feat_ref.shape[1]
    feat = feat_ref[...].reshape(rows, 512)
    cot = cot_ref[...].reshape(rows, 512)
    sent_ref[:, 0:512] = feat
    for group in range(4):
        taps = [weight_ref[8 * group + t] if 8 * group + t < 27 else jnp.zeros((16, 64), bf16) for t in range(8)]
        sent_ref[:, 512 + 64 * group : 576 + 64 * group] = jnp.concatenate(taps, axis=0)
    low = jnp.concatenate([feat[:, 0:64], cot[:, 0:64]], axis=1)
    high = jnp.concatenate([feat[:, 448:512], cot[:, 448:512]], axis=1)
    even = place_ref[0] % 2 == 0

    @pl.when(even)
    def _():
        first_ref[...] = high
        second_ref[...] = low

    @pl.when(jnp.logical_not(even))
    def _():
        first_ref[...] = low
        second_ref[...] = high


def kernel_grad_kernel(scale, place_ref, near_ref, got_ref, cot_ref, first_ref, second_ref, part_ref, sent_ref, padded, products):
    bricks = cot_ref.shape[0]
    rows = bricks * 16
    cot = cot_ref[...].reshape(rows, 512)
    even = jnp.full((rows, 128), place_ref[0] % 2, i32) == 0
    first, second = first_ref[...].astype(f32), second_ref[...].astype(f32)
    before = jnp.where(even, second, first)
    after = jnp.where(even, first, second)
    left = iota((rows, 128), 1) < 64
    sent_ref[:, 0:512] = cot
    sent_ref[:, 512:640] = jnp.where(left, before, pltpu.roll(after, 64, 1)).astype(bf16)
    sent_ref[:, 640:768] = jnp.where(left, pltpu.roll(before, 64, 1), after).astype(bf16)

    flat = jnp.transpose(cot.astype(f32)).astype(bf16)
    planes = [jnp.transpose(view)[64:128].astype(bf16) for view in (before, after)]
    near = near_ref[...]
    near = jnp.where(near < 0, bricks, near % bricks).astype(f32)
    widen = (iota((bricks, rows), 1) // 16 == iota((bricks, rows), 0)).astype(f32)
    source = lax.dot_general(near, widen, (((0,), (0,)), ((), ())), preferred_element_type=f32)
    source = source.astype(i32) * 16 + iota((27, rows), 1) % 16
    row_ids = iota((rows, rows), 0)
    edge = iota((1, 8, 128), 1)
    for i in range(3):
        for j in range(3):
            if i == 1:
                columns = flat.reshape(8, 8, 8, 128)
                if j != 1:
                    columns = columns[:, 7:8] if j == 0 else columns[:, 0:1]
            else:
                columns = planes[i // 2].reshape(1, 8, 8, 128)
                if j != 1:
                    columns = columns[:, 7:8] if j == 0 else columns[:, 0:1]
            wide, deep = columns.shape[0], columns.shape[1]
            count = wide * deep
            picks = [
                (row_ids == source[9 * i + 3 * j + k : 9 * i + 3 * j + k + 1, :]).astype(f32).astype(bf16)
                for k in range(3)
            ]
            moved = jnp.dot(columns.reshape(count * 8, 128), jnp.concatenate(picks, axis=1), preferred_element_type=f32)
            lower, own, upper = (moved[:, 128 * k : 128 * k + 128].reshape(count, 8, 128) for k in range(3))
            down = jnp.where(edge == 0, pltpu.roll(lower, 1, 1), pltpu.roll(own, 1, 1))
            up = jnp.where(edge == 7, pltpu.roll(upper, 7, 1), pltpu.roll(own, 7, 1))
            xs = (0, 1) if i == 0 else ((1, 9) if i == 1 else (9, 10))
            ys = (0, 1) if j == 0 else ((1, 9) if j == 1 else (9, 10))
            for c, value in enumerate((down, own, up)):
                padded[c, xs[0] : xs[1], ys[0] : ys[1]] = value.reshape(wide, deep, 8, 128)

    feat = got_ref[:, :, 0:512].reshape(4 * rows, 512)
    lane_group = iota((16, 128), 1) // 16
    sums = []
    for begin, end in ((0, 8), (8, 14), (14, 22), (22, 27)):
        for tap in range(begin, end, 2):
            windows = []
            for one in (tap, min(tap + 1, end - 1)):
                mirror = 26 - one
                a, b, c = mirror // 9, mirror // 3 % 3, mirror % 3
                windows.append(padded[c, a : a + 8, b : b + 8].reshape(512, 128).astype(bf16))
            both = jnp.dot(feat, jnp.concatenate(windows, axis=1), preferred_element_type=f32)
            products[tap - begin] = both[:, 0:128]
            products[tap - begin + 1] = both[:, 128:256]
        last = end - begin - 1
        blocks = []
        for quarter in range(4):
            total = None
            for shift in range(8):
                chosen = None
                for brick in range(bricks):
                    slot = min((brick + shift) % 8, last)
                    start = quarter * rows + brick * 16
                    block = products[slot, start : start + 16, :]
                    chosen = block if chosen is None else jnp.where(lane_group == brick, block, chosen)
                if shift:
                    chosen = pltpu.roll(chosen, 16 * shift, 1)
                total = chosen if total is None else total + chosen
            blocks.append(total)
        sums.append(jnp.concatenate(blocks, axis=0))
    part_ref[0:128] = jnp.transpose(jnp.concatenate([sums[0], sums[2]], axis=0)) * scale
    part_ref[128:224] = jnp.transpose(jnp.concatenate([sums[1], sums[3]], axis=0))[0:96] * scale


def pad_kernel(place_ref, near_ref, feat_ref, cot_ref, weight_ref, grid_ref, mat_ref, flat, planes, padded):
    bricks = near_ref.shape[0]
    for s in range(bricks):
        rows = slice(16 * s, 16 * s + 16)
        both = jnp.concatenate([feat_ref[q, rows, 0:512] for q in range(4)] + [cot_ref[q, rows, 0:512] for q in range(4)], axis=0)
        flat[512 * s : 512 * s + 512] = jnp.transpose(both.astype(f32))
        both = jnp.concatenate(
            [cot_ref[q, rows, 512:640] for q in range(4)] + [cot_ref[q, rows, 640:768] for q in range(4)], axis=0
        )
        planes[128 * s : 128 * s + 128] = jnp.transpose(both.astype(f32))
    flat[512 * bricks : 512 * bricks + 512] = jnp.zeros((512, 128), f32)
    planes[128 * bricks : 128 * bricks + 128] = jnp.zeros((128, 128), f32)

    for r in range(bricks):
        for i in range(3):
            for j in range(3):
                for k in range(3):
                    listed = near_ref[r, 9 * i + 3 * j + k]
                    s = jnp.where(listed < 0, bricks, listed % bricks)
                    source, base = (flat, s * 512) if i == 1 else (planes, s * 128 + (64 if i == 2 else 0))
                    x_pairs = [(x + 1, x) for x in range(8)] if i == 1 else [(0 if i == 0 else 9, 0)]
                    y_pairs = [(y + 1, y) for y in range(8)] if j == 1 else [(0, 7) if j == 0 else (9, 0)]
                    z_to, z_from = (1, 0) if k == 1 else ((0, 7) if k == 0 else (9, 0))
                    if k == 1:
                        for x_to, x_from in x_pairs:
                            for y_to, y_from in y_pairs:
                                piece = source[pl.ds(base + 64 * x_from + 8 * y_from, 8), :]
                                padded[pl.ds(80 * (10 * x_to + y_to) + 8 + r, 8, 8), :] = piece
                    elif j == 1:
                        for x_to, x_from in x_pairs:
                            piece = source[pl.ds(base + 64 * x_from + z_from, 8, 8), :]
                            padded[pl.ds(80 * (10 * x_to + 1) + 8 * z_to + r, 8, 80), :] = piece
                    elif i == 1:
                        piece = source[pl.ds(base + 8 * y_pairs[0][1] + z_from, 8, 64), :]
                        padded[pl.ds(80 * (10 + y_pairs[0][0]) + 8 * z_to + r, 8, 800), :] = piece
                    else:
                        piece = source[pl.ds(base + 8 * y_pairs[0][1] + z_from, 1), :]
                        padded[pl.ds(80 * (10 * x_pairs[0][0] + y_pairs[0][0]) + 8 * z_to + r, 1), :] = piece
    for x in range(10):
        grid_ref[800 * x : 800 * x + 800] = padded[800 * x : 800 * x + 800].astype(bf16)

    chan = place_ref[1]
    lanes = iota((48, 128), 1)
    spots = iota((48, 128), 0)
    forward = (lanes == 32 * (spots // 16) + spots % 16).astype(f32).astype(bf16)
    lanes = iota((256, 128), 1)
    spots = iota((256, 128), 0)
    picks = {}
    for group in range(4):
        for c in range(3):
            hit = (lanes - 32 * c - 16 == spots - 64 * group - 16 * chan) & (lanes >= 32 * c + 16) & (lanes < 32 * c + 32)
            picks[group, c] = hit.astype(f32).astype(bf16)
    for spot in range(9):
        own = weight_ref[3 * spot : 3 * spot + 3].reshape(48, 64)
        mat_ref[128 * spot : 128 * spot + 64] = lax.dot_general(
            own, forward, (((0,), (0,)), ((), ())), preferred_element_type=f32
        ).astype(bf16)
        total = None
        for c in range(3):
            tap = 26 - 3 * spot - c
            begin = 16 * (tap % 8)
            block = jnp.concatenate([feat_ref[q, begin : begin + 16, 512:768] for q in range(4)], axis=0)
            term = jnp.dot(block, picks[tap // 8, c], preferred_element_type=f32)
            total = term if total is None else total + term
        mat_ref[128 * spot + 64 : 128 * spot + 128] = total.astype(bf16)


def conv_kernel(grid_ref, mat_ref, out_ref, grad_ref, done):
    bricks = out_ref.shape[0]

    def layer(x, carry):
        pieces = []
        for a in range(3):
            for b in range(3):
                start = pl.multiple_of((x + a) * 800 + 80 * b, 16)
                pieces.append(grid_ref[pl.ds(start, 640), :])
        sums = jnp.dot(jnp.concatenate(pieces, axis=1), mat_ref[...], preferred_element_type=f32).reshape(8, 80, 128)
        total = sums[:, 0:64] + pltpu.roll(sums[:, 8:72], 96, 2) + pltpu.roll(sums[:, 16:80], 64, 2)
        done[pl.ds(pl.multiple_of(x * 512, 512), 512), :] = total.reshape(512, 128)
        return carry

    lax.fori_loop(0, 8, layer, 0)
    for r in range(bricks):
        turned = jnp.transpose(done[pl.ds(r, 512, 8), :])
        out_ref[r] = turned[0:16].astype(bf16)
        grad_ref[r] = turned[16:32].astype(bf16)


def finish_kernel(one_ref, other_ref, grad_ref):
    total = one_ref[...] + other_ref[...]
    for tap in range(27):
        slot = tap % 14
        block = total[16 * slot : 16 * slot + 16]
        grad_ref[tap] = block[:, 0:64] if tap < 14 else block[:, 64:128]


def body(features, weight, cotangent, neighbours):
    bricks, narrow = features.shape[0], features.shape[1]
    rows = bricks * narrow
    length = lax.axis_size("space")
    place = jnp.stack([lax.axis_index("space"), lax.axis_index("chan")]).astype(i32)
    shape = jax.ShapeDtypeStruct

    packed, first, second = call(
        prepare_kernel,
        (shape((rows, 768), bf16), shape((rows, 128), bf16), shape((rows, 128), bf16)),
        [],
        place, features, cotangent, weight,
        specs=[SMEM, VMEM, VMEM, VMEM],
    )
    ahead = [pair for i in range(0, length - 1, 2) for pair in ((i, i + 1), (i + 1, i))]
    behind = [pair for i in range(1, length - 1, 2) for pair in ((i, i + 1), (i + 1, i))]
    first = lax.ppermute(first, "space", ahead)
    second = lax.ppermute(second, "space", behind)
    got = lax.all_gather(packed, "chan", axis=0, tiled=False)

    scale = float(bricks * length * 512) ** -0.5
    part, packed = call(
        functools.partial(kernel_grad_kernel, scale),
        (shape((224, 128), f32), shape((rows, 768), bf16)),
        [pltpu.VMEM((3, 10, 10, 8, 128), f32), pltpu.VMEM((8, 4 * rows, 128), f32)],
        place, neighbours, got, cotangent, first, second,
        specs=[SMEM, VMEM, VMEM, VMEM, VMEM, VMEM],
    )
    steps = []
    step = 1
    while step < length:
        steps.append(step)
        step *= 2

    def partner(step):
        return lax.ppermute(part, "space", [(i, i ^ step) for i in range(length)])

    got_cot = lax.all_gather(packed, "chan", axis=0, tiled=False)
    for step in steps[:-1]:
        part = part + partner(step)
    grid, matrix = call(
        pad_kernel,
        (shape((8000, 128), bf16), shape((1152, 128), bf16)),
        [
            pltpu.VMEM(((bricks + 1) * 512, 128), f32),
            pltpu.VMEM(((bricks + 1) * 128, 128), f32),
            pltpu.VMEM((8000, 128), f32),
        ],
        place, neighbours, got, got_cot, weight,
        specs=[SMEM, SMEM, VMEM, VMEM, VMEM],
    )
    output, grad_input = call(
        conv_kernel,
        (shape(features.shape, bf16), shape(features.shape, bf16)),
        [pltpu.VMEM((4096, 128), f32)],
        grid, matrix,
        specs=[VMEM, VMEM],
    )
    grad_weight = call(
        finish_kernel, shape(weight.shape, f32), [], part, partner(steps[-1]), specs=[VMEM, VMEM]
    )
    return (output, grad_input, grad_weight)


def solution(mesh):
    in_specs = (
        P("space", "chan", None),
        P(None, "chan", None),
        P("space", "chan", None),
        P("space", None),
    )
    out_specs = (P("space", "chan", None), P("space", "chan", None), P(None, "chan", None))
    return jax.shard_map(body, mesh=mesh, in_specs=in_specs, out_specs=out_specs, check_vma=False)
```

```python
import functools

import jax
import jax.numpy as jnp
from jax import lax
from jax.experimental import pallas as pl
from jax.experimental.pallas import tpu as pltpu
from jax.sharding import PartitionSpec as P

f32, bf16, i32 = jnp.float32, jnp.bfloat16, jnp.int32
VMEM = pl.BlockSpec(memory_space=pltpu.VMEM)
HBM = pl.BlockSpec(memory_space=pltpu.HBM)
SMEM = pl.BlockSpec(memory_space=pltpu.SMEM)

GROUPS = ((0, 8), (8, 14), (14, 22), (22, 27))


def iota(shape, axis):
    return lax.broadcasted_iota(i32, shape, axis)


def call(kernel, out_shape, scratch, *args, specs, limit=48 << 20):
    return pl.pallas_call(
        kernel,
        out_shape=out_shape,
        in_specs=specs,
        out_specs=jax.tree.map(lambda _: VMEM, out_shape),
        scratch_shapes=scratch,
        compiler_params=pltpu.CompilerParams(vmem_limit_bytes=limit),
    )(*args)


def prepare_kernel(feat_any, cot_any, weight_any, near_any, feat_ref, cot_ref, weight_ref, near_ref, first_ref, second_ref, sems):
    rows = first_ref.shape[0]
    pairs = ((feat_any, feat_ref), (cot_any, cot_ref), (weight_any, weight_ref), (near_any, near_ref))
    copies = [pltpu.make_async_copy(source, target, sems.at[i]) for i, (source, target) in enumerate(pairs)]
    for copy in copies:
        copy.start()
    for copy in copies[:2]:
        copy.wait()
    low = jnp.concatenate([view[:, :, 0:64].reshape(rows, 64) for view in (feat_ref, cot_ref)], axis=1)
    high = jnp.concatenate([view[:, :, 448:512].reshape(rows, 64) for view in (feat_ref, cot_ref)], axis=1)
    even = lax.axis_index("space") % 2 == 0

    @pl.when(even)
    def _():
        first_ref[...] = high
        second_ref[...] = low

    @pl.when(jnp.logical_not(even))
    def _():
        first_ref[...] = low
        second_ref[...] = high

    for copy in copies[2:]:
        copy.wait()


def pack_kernel(cot_ref, weight_ref, first_ref, second_ref, sent_ref):
    rows = first_ref.shape[0]
    even = jnp.full((rows, 128), lax.axis_index("space") % 2, i32) == 0
    first, second = first_ref[...].astype(f32), second_ref[...].astype(f32)
    before = jnp.where(even, second, first)
    after = jnp.where(even, first, second)
    left = iota((rows, 128), 1) < 64
    sent_ref[:, 0:512] = cot_ref[...].reshape(rows, 512)
    sent_ref[:, 512:640] = jnp.where(left, before, pltpu.roll(after, 64, 1)).astype(bf16)
    sent_ref[:, 640:768] = jnp.where(left, pltpu.roll(before, 64, 1), after).astype(bf16)
    for group in range(4):
        taps = [weight_ref[8 * group + t] if 8 * group + t < 27 else jnp.zeros((16, 64), bf16) for t in range(8)]
        sent_ref[:, 768 + 64 * group : 832 + 64 * group] = jnp.concatenate(taps, axis=0)


def tap_sums(views, windows, bricks, products):
    rows = bricks * 16
    feat = jnp.concatenate([view[...].reshape(rows, 512) for view in views], axis=0)
    lane_group = iota((16, 128), 1) // 16
    sums = []
    pair = 0
    for begin, end in GROUPS:
        for tap in range(begin, end, 2):
            both = jnp.dot(feat, windows(pair, tap, min(tap + 1, end - 1)), preferred_element_type=f32)
            products[tap - begin] = both[:, 0:128]
            products[tap - begin + 1] = both[:, 128:256]
            pair += 1
        last = end - begin - 1
        blocks = []
        for index in range(len(views)):
            total = None
            for shift in range(8):
                chosen = None
                for brick in range(bricks):
                    start = index * rows + brick * 16
                    block = products[min((brick + shift) % 8, last), start : start + 16, :]
                    chosen = block if chosen is None else jnp.where(lane_group == brick, block, chosen)
                if shift:
                    chosen = pltpu.roll(chosen, 16 * shift, 1)
                total = chosen if total is None else total + chosen
            blocks.append(total)
        sums.append(blocks)
    return sums


def near_grad_kernel(near_ref, packed_ref, feat_ref, feat1_ref, windows_ref, sums_ref, padded, products):
    rows = packed_ref.shape[0]
    flat = jnp.transpose(packed_ref[:, 0:512].astype(f32)).astype(bf16)
    planes = jnp.transpose(packed_ref[:, 640:768].astype(f32)).astype(bf16)
    bricks = near_ref.shape[0]
    listed = near_ref[...]
    listed = jnp.where(listed < 0, bricks, listed % bricks).astype(f32)
    widen = (iota((bricks, rows), 1) // 16 == iota((bricks, rows), 0)).astype(f32)
    source = lax.dot_general(listed, widen, (((0,), (0,)), ((), ())), preferred_element_type=f32)
    source = source.astype(i32) * 16 + iota((27, rows), 1) % 16
    row_ids = iota((rows, rows), 0)
    edge = iota((1, 8, 128), 1)
    for i in range(3):
        for j in range(3):
            columns = flat.reshape(8, 8, 8, 128) if i == 1 else planes[32 * i : 32 * i + 64].reshape(1, 8, 8, 128)
            if j != 1:
                columns = columns[:, 7:8] if j == 0 else columns[:, 0:1]
            wide, deep = columns.shape[0], columns.shape[1]
            count = wide * deep
            picks = [
                (row_ids == source[9 * i + 3 * j + k : 9 * i + 3 * j + k + 1, :]).astype(f32).astype(bf16)
                for k in range(3)
            ]
            moved = jnp.dot(columns.reshape(count * 8, 128), jnp.concatenate(picks, axis=1), preferred_element_type=f32)
            lower, own, upper = (moved[:, 128 * k : 128 * k + 128].reshape(count, 8, 128) for k in range(3))
            down = jnp.where(edge == 0, pltpu.roll(lower, 1, 1), pltpu.roll(own, 1, 1))
            up = jnp.where(edge == 7, pltpu.roll(upper, 7, 1), pltpu.roll(own, 7, 1))
            xs = (0, 1) if i == 0 else ((1, 9) if i == 1 else (9, 10))
            ys = (0, 1) if j == 0 else ((1, 9) if j == 1 else (9, 10))
            for c, value in enumerate((down, own, up)):
                padded[c, xs[0] : xs[1], ys[0] : ys[1]] = value.reshape(wide, deep, 8, 128)

    def windows(pair, *taps):
        views = []
        for tap in taps:
            a, b, c = (26 - tap) // 9, (26 - tap) // 3 % 3, (26 - tap) % 3
            views.append(padded[c, a : a + 8, b : b + 8].reshape(512, 128).astype(bf16))
        both = jnp.concatenate(views, axis=1)
        windows_ref[pair] = both
        return both

    sums = tap_sums((feat_ref, feat1_ref), windows, feat_ref.shape[0], products)
    for group in range(4):
        sums_ref[group] = jnp.concatenate(sums[group], axis=0)


def far_grad_kernel(scale, windows_ref, feat2_ref, feat3_ref, sums_ref, part_ref, products, ordered):
    chan = lax.axis_index("chan")
    sums = tap_sums((feat2_ref, feat3_ref), lambda pair, *taps: windows_ref[pair], feat2_ref.shape[0], products)
    for group in range(4):
        both = sums_ref[group]
        for apart, block in enumerate((both[0:16], both[16:32], *sums[group])):
            ordered[group, pl.ds(pl.multiple_of(16 * (chan ^ apart), 16), 16), :] = block
    part_ref[0:128] = jnp.transpose(jnp.concatenate([ordered[0], ordered[2]], axis=0)) * scale
    part_ref[128:224] = jnp.transpose(jnp.concatenate([ordered[1], ordered[3]], axis=0))[0:96] * scale


def pad_kernel(near_ref, weight_ref, *refs):
    feats, cots, (grid_ref, mat_ref, flat, planes, padded) = refs[:4], refs[4:8], refs[8:]
    bricks = near_ref.shape[0]
    for s in range(bricks):
        rows = slice(16 * s, 16 * s + 16)
        both = jnp.concatenate([feat[s] for feat in feats] + [cot[rows, 0:512] for cot in cots], axis=0)
        flat[512 * s : 512 * s + 512] = jnp.transpose(both.astype(f32))
        both = jnp.concatenate([cot[rows, 512:640] for cot in cots] + [cot[rows, 640:768] for cot in cots], axis=0)
        planes[128 * s : 128 * s + 128] = jnp.transpose(both.astype(f32))
    flat[512 * bricks : 512 * bricks + 512] = jnp.zeros((512, 128), f32)
    planes[128 * bricks : 128 * bricks + 128] = jnp.zeros((128, 128), f32)

    for r in range(bricks):
        for i in range(3):
            for j in range(3):
                for k in range(3):
                    listed = near_ref[r, 9 * i + 3 * j + k]
                    s = jnp.where(listed < 0, bricks, listed % bricks)
                    source, base = (flat, s * 512) if i == 1 else (planes, s * 128 + (64 if i == 2 else 0))
                    x_pairs = [(x + 1, x) for x in range(8)] if i == 1 else [(0 if i == 0 else 9, 0)]
                    y_pairs = [(y + 1, y) for y in range(8)] if j == 1 else [(0, 7) if j == 0 else (9, 0)]
                    z_to, z_from = (1, 0) if k == 1 else ((0, 7) if k == 0 else (9, 0))
                    if k == 1:
                        for x_to, x_from in x_pairs:
                            for y_to, y_from in y_pairs:
                                piece = source[pl.ds(base + 64 * x_from + 8 * y_from, 8), :]
                                padded[pl.ds(80 * (10 * x_to + y_to) + 8 + r, 8, 8), :] = piece
                    elif j == 1:
                        for x_to, x_from in x_pairs:
                            piece = source[pl.ds(base + 64 * x_from + z_from, 8, 8), :]
                            padded[pl.ds(80 * (10 * x_to + 1) + 8 * z_to + r, 8, 80), :] = piece
                    elif i == 1:
                        piece = source[pl.ds(base + 8 * y_pairs[0][1] + z_from, 8, 64), :]
                        padded[pl.ds(80 * (10 + y_pairs[0][0]) + 8 * z_to + r, 8, 800), :] = piece
                    else:
                        piece = source[pl.ds(base + 8 * y_pairs[0][1] + z_from, 1), :]
                        padded[pl.ds(80 * (10 * x_pairs[0][0] + y_pairs[0][0]) + 8 * z_to + r, 1), :] = piece
    for x in range(10):
        grid_ref[800 * x : 800 * x + 800] = padded[800 * x : 800 * x + 800].astype(bf16)

    chan = lax.axis_index("chan")
    lanes = iota((48, 128), 1)
    spots = iota((48, 128), 0)
    forward = (lanes == 32 * (spots // 16) + spots % 16).astype(f32).astype(bf16)
    lanes = iota((256, 128), 1)
    spots = iota((256, 128), 0)
    picks = {}
    for group in range(4):
        for c in range(3):
            hit = (lanes - 32 * c - 16 == spots - 64 * group - 16 * chan) & (lanes >= 32 * c + 16) & (lanes < 32 * c + 32)
            picks[group, c] = hit.astype(f32).astype(bf16)
    for spot in range(9):
        own = weight_ref[3 * spot : 3 * spot + 3].reshape(48, 64)
        turned = lax.dot_general(own, forward, (((0,), (0,)), ((), ())), preferred_element_type=f32).astype(bf16)
        for q in range(4):
            mat_ref[pl.ds(pl.multiple_of(128 * spot + 16 * (chan ^ q), 16), 16), :] = turned[16 * q : 16 * q + 16]
        total = None
        for c in range(3):
            tap = 26 - 3 * spot - c
            begin = 16 * (tap % 8)
            block = jnp.concatenate([cot[begin : begin + 16, 768:1024] for cot in cots], axis=0)
            term = jnp.dot(block, picks[tap // 8, c], preferred_element_type=f32)
            total = term if total is None else total + term
        mat_ref[128 * spot + 64 : 128 * spot + 128] = total.astype(bf16)


def conv_layers(grid_ref, mat_ref, done, first, last):
    def layer(x, carry):
        pieces = []
        for a in range(3):
            for b in range(3):
                start = pl.multiple_of((x + a) * 800 + 80 * b, 16)
                pieces.append(grid_ref[pl.ds(start, 640), :])
        sums = jnp.dot(jnp.concatenate(pieces, axis=1), mat_ref[...], preferred_element_type=f32).reshape(8, 80, 128)
        total = sums[:, 0:64] + pltpu.roll(sums[:, 8:72], 96, 2) + pltpu.roll(sums[:, 16:80], 64, 2)
        done[pl.ds(pl.multiple_of((x - first) * 512, 512), 512), :] = total.reshape(512, 128)
        return carry

    lax.fori_loop(first, last, layer, 0)


def low_kernel(grid_ref, mat_ref, done_ref):
    conv_layers(grid_ref, mat_ref, done_ref, 0, 4)


def high_kernel(grid_ref, mat_ref, low_ref, out_ref, grad_ref, done):
    conv_layers(grid_ref, mat_ref, done, 4, 8)
    for r in range(out_ref.shape[0]):
        turned = jnp.transpose(jnp.concatenate([view[pl.ds(r, 256, 8), :] for view in (low_ref, done)], axis=0))
        out_ref[r] = turned[0:16].astype(bf16)
        grad_ref[r] = turned[16:32].astype(bf16)


def finish_kernel(one_ref, other_ref, grad_ref):
    total = one_ref[...] + other_ref[...]
    for tap in range(27):
        slot = tap % 14
        block = total[16 * slot : 16 * slot + 16]
        grad_ref[tap] = block[:, 0:64] if tap < 14 else block[:, 64:128]


def body(features, weight, cotangent, neighbours):
    bricks, narrow = features.shape[0], features.shape[1]
    rows = bricks * narrow
    length = lax.axis_size("space")
    shape = jax.ShapeDtypeStruct

    def across(value, apart, axis="chan"):
        return lax.ppermute(value, axis, [(i, i ^ apart) for i in range(lax.axis_size(axis))])

    feat2 = across(features, 2)
    feat1 = across(features, 1)
    inputs = (features, cotangent, weight, neighbours)
    feat, cot, kernel_rows, near, first, second = call(
        prepare_kernel,
        tuple(shape(view.shape, view.dtype) for view in inputs) + (shape((rows, 128), bf16), shape((rows, 128), bf16)),
        [pltpu.SemaphoreType.DMA((4,))],
        *(pltpu.with_memory_space_constraint(view, pltpu.HBM) for view in inputs),
        specs=[HBM] * 4,
    )
    ahead = [pair for i in range(0, length - 1, 2) for pair in ((i, i + 1), (i + 1, i))]
    behind = [pair for i in range(1, length - 1, 2) for pair in ((i, i + 1), (i + 1, i))]
    first = lax.ppermute(first, "space", ahead)
    second = lax.ppermute(second, "space", behind)
    first, second, feat2 = lax.optimization_barrier((first, second, feat2))
    packed = call(
        pack_kernel, shape((rows, 1024), bf16), [], cot, kernel_rows, first, second, specs=[VMEM] * 4
    )
    packed2 = across(packed, 2)
    packed1 = across(packed, 1)
    feat3 = across(feat2, 1)
    windows, sums = call(
        near_grad_kernel,
        (shape((14, 512, 256), bf16), shape((4, 32, 128), f32)),
        [pltpu.VMEM((3, 10, 10, 8, 128), f32), pltpu.VMEM((8, 2 * rows, 128), f32)],
        near, packed, feat, feat1,
        specs=[VMEM] * 4,
    )
    part = call(
        functools.partial(far_grad_kernel, float(bricks * length * 512) ** -0.5),
        shape((224, 128), f32),
        [pltpu.VMEM((8, 2 * rows, 128), f32), pltpu.VMEM((4, 64, 128), f32)],
        windows, feat2, feat3, sums,
        specs=[VMEM] * 4,
    )
    packed2, part = lax.optimization_barrier((packed2, part))
    packed3 = across(packed2, 1)
    steps = []
    step = 1
    while step < length:
        steps.append(step)
        step *= 2
    grid, matrix = call(
        pad_kernel,
        (shape((8000, 128), bf16), shape((1152, 128), bf16)),
        [
            pltpu.VMEM(((bricks + 1) * 512, 128), f32),
            pltpu.VMEM(((bricks + 1) * 128, 128), f32),
            pltpu.VMEM((8000, 128), f32),
        ],
        near, kernel_rows, feat, feat1, feat2, feat3, packed, packed1, packed2, packed3,
        specs=[SMEM] + [VMEM] * 9,
    )
    other = across(part, steps[0], "space")
    for step in steps[1:-1]:
        other, grid, matrix = lax.optimization_barrier((other, grid, matrix))
        part = part + other
        other = across(part, step, "space")
    low = call(low_kernel, shape((2048, 128), f32), [], grid, matrix, specs=[VMEM, VMEM])
    other, low = lax.optimization_barrier((other, low))
    part = part + other
    other = across(part, steps[-1], "space")
    output, grad_input = call(
        high_kernel,
        (shape(features.shape, bf16), shape(features.shape, bf16)),
        [pltpu.VMEM((2048, 128), f32)],
        grid, matrix, low,
        specs=[VMEM, VMEM, VMEM],
    )
    other, output, grad_input = lax.optimization_barrier((other, output, grad_input))
    grad_weight = call(finish_kernel, shape(weight.shape, f32), [], part, other, specs=[VMEM, VMEM])
    return (output, grad_input, grad_weight)


def solution(mesh):
    in_specs = (
        P("space", "chan", None),
        P(None, "chan", None),
        P("space", "chan", None),
        P("space", None),
    )
    out_specs = (P("space", "chan", None), P("space", "chan", None), P(None, "chan", None))
    return jax.shard_map(body, mesh=mesh, in_specs=in_specs, out_specs=out_specs, check_vma=False)
```

```python
import functools

import jax
import jax.numpy as jnp
from jax import lax
from jax.experimental import pallas as pl
from jax.experimental.pallas import tpu as pltpu
from jax.sharding import PartitionSpec as P

f32, bf16, i32 = jnp.float32, jnp.bfloat16, jnp.int32
VMEM = pl.BlockSpec(memory_space=pltpu.VMEM)
HBM = pl.BlockSpec(memory_space=pltpu.HBM)

COSTS = {}
GROUPS = ((0, 8), (8, 14), (14, 22), (22, 27))


def iota(shape, axis):
    return lax.broadcasted_iota(i32, shape, axis)


def call(kernel, out_shape, scratch, *args, specs):
    name = getattr(kernel, "func", kernel).__name__
    return pl.pallas_call(
        kernel,
        name=name,
        out_shape=out_shape,
        in_specs=specs,
        out_specs=jax.tree.map(lambda _: VMEM, out_shape),
        scratch_shapes=scratch,
        compiler_params=pltpu.CompilerParams(vmem_limit_bytes=48 << 20),
        cost_estimate=pl.CostEstimate(flops=COSTS.get(name, 0), bytes_accessed=0, transcendentals=0),
    )(*args)


def prepare_kernel(feat_any, cot_any, weight_any, near_any, both_ref, weight_ref, near_ref, first_ref, second_ref, sems):
    rows = first_ref.shape[0]
    pairs = (
        (feat_any, both_ref.at[:, :, 0:512]),
        (cot_any, both_ref.at[:, :, 512:1024]),
        (weight_any, weight_ref),
        (near_any, near_ref),
    )
    copies = [pltpu.make_async_copy(source, target, sems.at[i]) for i, (source, target) in enumerate(pairs)]
    for copy in copies:
        copy.start()
    for copy in copies[:2]:
        copy.wait()
    low = jnp.concatenate([both_ref[:, :, i : i + 64].reshape(rows, 64) for i in (0, 512)], axis=1)
    high = jnp.concatenate([both_ref[:, :, i : i + 64].reshape(rows, 64) for i in (448, 960)], axis=1)
    even = lax.axis_index("space") % 2 == 0

    @pl.when(even)
    def _():
        first_ref[...] = high
        second_ref[...] = low

    @pl.when(jnp.logical_not(even))
    def _():
        first_ref[...] = low
        second_ref[...] = high

    for copy in copies[2:]:
        copy.wait()


def pack_kernel(both_ref, weight_ref, first_ref, second_ref, near_pack_ref, far_pack_ref):
    rows = first_ref.shape[0]
    even = jnp.full((rows, 128), lax.axis_index("space") % 2, i32) == 0
    first, second = first_ref[...].astype(f32), second_ref[...].astype(f32)
    before = jnp.where(even, second, first)
    after = jnp.where(even, first, second)
    left = iota((rows, 128), 1) < 64
    feat = jnp.where(left, before, pltpu.roll(after, 64, 1)).astype(bf16)
    cot = jnp.where(left, pltpu.roll(before, 64, 1), after).astype(bf16)
    groups = []
    for group in range(4):
        taps = [weight_ref[8 * group + t] if 8 * group + t < 27 else jnp.zeros((16, 64), bf16) for t in range(8)]
        groups.append(jnp.concatenate(taps, axis=0))
    kernel = jnp.concatenate(groups, axis=1)
    spots, lanes = iota((256, 128), 0), iota((256, 128), 1)
    place = lax.axis_index("chan") // 2
    for target, pair in ((near_pack_ref, place), (far_pack_ref, place ^ 1)):
        target[:, 0:128] = feat
        target[:, 128:256] = cot
        owned = spots == 64 * (lanes // 32) + 32 * pair + lanes % 32
        part = jnp.dot(kernel, owned.astype(f32).astype(bf16), preferred_element_type=f32)
        target[:, 256:384] = part.astype(bf16)
    far_pack_ref[:, 384:896] = both_ref[:, :, 512:1024].reshape(rows, 512)


def tap_sums(products, count, bricks):
    lane_group = iota((16, 128), 1) // 16
    sums = []
    for begin, end in GROUPS:
        blocks = []
        for view in range(count):
            total = None
            for shift in range(8):
                chosen = None
                for brick in range(bricks):
                    start = (view * bricks + brick) * 16
                    block = products[min(begin + (brick + shift) % 8, end - 1), start : start + 16, :]
                    chosen = block if chosen is None else jnp.where(lane_group == brick, block, chosen)
                if shift:
                    chosen = pltpu.roll(chosen, 16 * shift, 1)
                total = chosen if total is None else total + chosen
            blocks.append(total)
        sums.append(blocks)
    return sums


def brick_picker(near_ref, rows):
    bricks = near_ref.shape[0]
    listed = near_ref[...]
    listed = jnp.where(listed < 0, bricks, listed % bricks).astype(f32)
    widen = (iota((bricks, rows), 1) // 16 == iota((bricks, rows), 0)).astype(f32)
    source = lax.dot_general(listed, widen, (((0,), (0,)), ((), ())), preferred_element_type=f32)
    source = source.astype(i32) * 16 + iota((27, rows), 1) % 16
    row_ids = iota((rows, rows), 0)

    def pick(i, j):
        first = 9 * i + 3 * j
        picks = [(row_ids == source[first + k : first + k + 1, :]).astype(f32).astype(bf16) for k in range(3)]
        return jnp.concatenate(picks, axis=1)

    return pick


def shifted_columns(columns, pick, j):
    if j != 1:
        columns = columns[:, 7:8] if j == 0 else columns[:, 0:1]
    wide, deep = columns.shape[0], columns.shape[1]
    count = wide * deep
    edge = iota((1, 8, 128), 1)
    moved = jnp.dot(columns.reshape(count * 8, 128), pick, preferred_element_type=f32)
    lower, own, upper = (moved[:, 128 * k : 128 * k + 128].reshape(count, 8, 128) for k in range(3))
    down = jnp.where(edge == 0, pltpu.roll(lower, 1, 1), pltpu.roll(own, 1, 1))
    up = jnp.where(edge == 7, pltpu.roll(upper, 7, 1), pltpu.roll(own, 7, 1))
    return [value.reshape(wide, deep, 8, 128) for value in (down, own, up)]


ROWS_TO = ((0, 1), (1, 9), (9, 10))


def near_grad_kernel(near_ref, both_ref, both1_ref, windows_ref, sums_ref, padded, products):
    bricks = near_ref.shape[0]
    rows = bricks * 16
    flat = jnp.transpose(both_ref[:, :, 512:1024].reshape(rows, 512).astype(f32)).astype(bf16).reshape(8, 8, 8, 128)
    pick = brick_picker(near_ref, rows)
    for x in (0, 9):
        padded[:, x] = jnp.zeros((3, 10, 8, 128), f32)
    for j in range(3):
        for c, value in enumerate(shifted_columns(flat, pick(1, j), j)):
            padded[c, 1:9, ROWS_TO[j][0] : ROWS_TO[j][1]] = value
    feat = jnp.concatenate([view[:, :, 0:512].reshape(rows, 512) for view in (both_ref, both1_ref)], axis=0)
    for pair in range(14):
        views = []
        for tap in (2 * pair, min(2 * pair + 1, 26)):
            a, b, c = (26 - tap) // 9, (26 - tap) // 3 % 3, (26 - tap) % 3
            views.append(padded[c, a : a + 8, b : b + 8].reshape(512, 128).astype(bf16))
        window = jnp.concatenate(views, axis=1)
        windows_ref[pair] = window
        both = jnp.dot(feat, window, preferred_element_type=f32)
        products[2 * pair] = both[:, 0:128]
        products[2 * pair + 1] = both[:, 128:256]
    sums = tap_sums(products, 2, bricks)
    for group in range(4):
        sums_ref[group] = jnp.concatenate(sums[group], axis=0)


def plane_ends(views, side):
    rows = views[0].shape[0] * 16
    start = 0 if side == 0 else 448
    return jnp.concatenate([view[:, :, start : start + 64].reshape(rows, 64) for view in views], axis=0)


def halo_grad_kernel(near_ref, packed_ref, both_ref, both1_ref, sums_ref, windows_ref, total_ref, edges, products):
    bricks = near_ref.shape[0]
    rows = bricks * 16
    planes = jnp.transpose(packed_ref[:, 128:256].astype(f32)).astype(bf16)
    pick = brick_picker(near_ref, rows)
    for side in range(2):
        columns = planes[64 * side : 64 * side + 64].reshape(1, 8, 8, 128)
        for j in range(3):
            for c, value in enumerate(shifted_columns(columns, pick(2 * side, j), j)):
                edges[side, c, ROWS_TO[j][0] : ROWS_TO[j][1]] = value.reshape(value.shape[1:])
    for side in range(2):
        views = []
        for place in range(9):
            b, c = (8 - place) // 3, (8 - place) % 3
            views.append(edges[side, c, b : b + 8].reshape(64, 128).astype(bf16))
        window = jnp.concatenate(views, axis=1)
        windows_ref[side] = window
        both = jnp.dot(plane_ends([both_ref, both1_ref], side), window, preferred_element_type=f32)
        for place in range(9):
            products[18 * (1 - side) + place] = both[:, 128 * place : 128 * place + 128]
    for place in range(9, 18):
        products[place] = jnp.zeros((2 * rows, 128), f32)
    sums = tap_sums(products, 2, bricks)
    for group in range(4):
        total_ref[group] = sums_ref[group] + jnp.concatenate(sums[group], axis=0)


def far_grad_kernel(scale, windows_ref, edge_windows_ref, feat2_ref, feat3_ref, sums_ref, part_ref, products, ordered):
    chan = lax.axis_index("chan")
    bricks = feat2_ref.shape[0]
    rows = bricks * 16
    views = [feat2_ref, feat3_ref]
    for side in range(2):
        both = jnp.dot(plane_ends(views, side), edge_windows_ref[side], preferred_element_type=f32)
        for place in range(9):
            products[18 * (1 - side) + place] = both[:, 128 * place : 128 * place + 128]
    far = jnp.concatenate([view[...].reshape(rows, 512) for view in views], axis=0)
    for pair in range(14):
        both = jnp.dot(far, windows_ref[pair], preferred_element_type=f32)
        for tap in range(2 * pair, min(2 * pair + 2, 27)):
            one = both[:, 128 * (tap % 2) : 128 * (tap % 2) + 128]
            products[tap] = one if 9 <= tap < 18 else one + products[tap]
    sums = tap_sums(products, 2, bricks)
    for group in range(4):
        both = sums_ref[group]
        for apart, block in enumerate((both[0:16], both[16:32], *sums[group])):
            ordered[group, pl.ds(pl.multiple_of(16 * (chan ^ apart), 16), 16), :] = block
    part_ref[0:128] = jnp.transpose(jnp.concatenate([ordered[0], ordered[2]], axis=0)) * scale
    part_ref[128:224] = jnp.transpose(jnp.concatenate([ordered[1], ordered[3]], axis=0))[0:96] * scale


def pad_bricks(near, padded, source, size, xs):
    bricks = near.shape[0]
    for r in range(bricks):
        for i, base, x_pairs in xs:
            for j in range(3):
                for k in range(3):
                    listed = near[r, 9 * i + 3 * j + k]
                    start = jnp.where(listed < 0, bricks, listed % bricks) * size + base
                    y_pairs = [(y + 1, y) for y in range(8)] if j == 1 else [(0, 7) if j == 0 else (9, 0)]
                    z_to, z_from = (1, 0) if k == 1 else ((0, 7) if k == 0 else (9, 0))
                    if k == 1:
                        for x_to, x_from in x_pairs:
                            for y_to, y_from in y_pairs:
                                piece = source[pl.ds(start + 64 * x_from + 8 * y_from, 8), :]
                                padded[pl.ds(80 * (10 * x_to + y_to) + 8 + r, 8, 8), :] = piece
                    elif j == 1:
                        for x_to, x_from in x_pairs:
                            piece = source[pl.ds(start + 64 * x_from + z_from, 8, 8), :]
                            padded[pl.ds(80 * (10 * x_to + 1) + 8 * z_to + r, 8, 80), :] = piece
                    elif i == 1:
                        piece = source[pl.ds(start + 8 * y_pairs[0][1] + z_from, 8, 64), :]
                        padded[pl.ds(80 * y_pairs[0][0] + 8 * z_to + r, 8, 800), :] = piece
                    else:
                        piece = source[pl.ds(start + 8 * y_pairs[0][1] + z_from, 1), :]
                        padded[pl.ds(80 * (10 * x_pairs[0][0] + y_pairs[0][0]) + 8 * z_to + r, 1), :] = piece


def inner_kernel(near_ref, weight_ref, *refs):
    both, both1, feat2, feat3 = refs[:4]
    packs, (grid_ref, mat_ref, flat, padded, near, sem) = refs[4:8], refs[8:]
    copy = pltpu.make_async_copy(near_ref, near, sem)
    copy.start()
    bricks = feat2.shape[0]
    feats = [both.at[:, :, 0:512], both1.at[:, :, 0:512], feat2, feat3]
    cots = [both.at[:, :, 512:1024], both1.at[:, :, 512:1024]]
    for s in range(bricks):
        rows = slice(16 * s, 16 * s + 16)
        views = [view[s] for view in feats + cots] + [pack[rows, 384:896] for pack in packs[2:]]
        flat[512 * s : 512 * s + 512] = jnp.transpose(jnp.concatenate(views, axis=0).astype(f32))
    flat[512 * bricks : 512 * bricks + 512] = jnp.zeros((512, 128), f32)

    chan = lax.axis_index("chan")
    lanes = iota((48, 128), 1)
    spots = iota((48, 128), 0)
    forward = (lanes == 32 * (spots // 16) + spots % 16).astype(f32).astype(bf16)
    lanes = iota((128, 128), 1)
    spots = iota((128, 128), 0)
    picks = {}
    for group in range(4):
        for c in range(3):
            hit = lanes - 32 * c - 16 == spots - 32 * group - 16 * (chan % 2)
            hit = hit & (lanes >= 32 * c + 16) & (lanes < 32 * c + 32)
            picks[group, c] = hit.astype(f32).astype(bf16)
    for spot in range(9):
        own = weight_ref[3 * spot : 3 * spot + 3].reshape(48, 64)
        turned = lax.dot_general(own, forward, (((0,), (0,)), ((), ())), preferred_element_type=f32).astype(bf16)
        for q in range(4):
            mat_ref[pl.ds(pl.multiple_of(128 * spot + 16 * (chan ^ q), 16), 16), :] = turned[16 * q : 16 * q + 16]
        total = None
        for c in range(3):
            tap = 26 - 3 * spot - c
            block = jnp.concatenate([pack[16 * (tap % 8) : 16 * (tap % 8) + 16, 256:384] for pack in packs], axis=0)
            term = jnp.dot(block, picks[tap // 8, c], preferred_element_type=f32)
            total = term if total is None else total + term
        mat_ref[128 * spot + 64 : 128 * spot + 128] = total.astype(bf16)

    copy.wait()
    pad_bricks(near, padded, flat, 512, [(1, 0, [(x, x) for x in range(8)])])
    for x in range(8):
        grid_ref[800 * x : 800 * x + 800] = padded[800 * x : 800 * x + 800].astype(bf16)


def conv_layer(views, mat_ref):
    pieces = [view[80 * b : 80 * b + 640, :] for view in views for b in range(3)]
    sums = jnp.dot(jnp.concatenate(pieces, axis=1), mat_ref[...], preferred_element_type=f32).reshape(8, 80, 128)
    total = sums[:, 0:64] + pltpu.roll(sums[:, 8:72], 96, 2) + pltpu.roll(sums[:, 16:80], 64, 2)
    return total.reshape(512, 128)


def middle_kernel(grid_ref, mat_ref, done_ref):
    def layer(x, carry):
        views = [grid_ref.at[pl.ds(pl.multiple_of(800 * (x + a), 16), 800)] for a in range(3)]
        done_ref[pl.ds(pl.multiple_of(512 * x, 512), 512), :] = conv_layer(views, mat_ref)
        return carry

    lax.fori_loop(0, 6, layer, 0)


def outer_kernel(near_ref, grid_ref, mat_ref, middle_ref, *refs):
    packs, (out_ref, grad_ref, planes, padded, edges, low, high, near, sem) = refs[:4], refs[4:]
    copy = pltpu.make_async_copy(near_ref, near, sem)
    copy.start()
    bricks = near_ref.shape[0]
    for s in range(bricks):
        rows = slice(16 * s, 16 * s + 16)
        pair = jnp.concatenate([pack[rows, 0:128] for pack in packs] + [pack[rows, 128:256] for pack in packs], axis=0)
        planes[128 * s : 128 * s + 128] = jnp.transpose(pair.astype(f32))
    planes[128 * bricks : 128 * bricks + 128] = jnp.zeros((128, 128), f32)
    copy.wait()
    pad_bricks(near, padded, planes, 128, [(0, 0, [(0, 0)]), (2, 64, [(1, 0)])])
    edges[...] = padded[...].astype(bf16)
    layers = [edges.at[0:800]] + [grid_ref.at[800 * x : 800 * x + 800] for x in (0, 1, 6, 7)] + [edges.at[800:1600]]
    low[...] = conv_layer(layers[0:3], mat_ref)
    high[...] = conv_layer(layers[3:6], mat_ref)
    for r in range(bricks):
        views = [low[pl.ds(r, 64, 8), :], middle_ref[pl.ds(r, 384, 8), :], high[pl.ds(r, 64, 8), :]]
        turned = jnp.transpose(jnp.concatenate(views, axis=0))
        out_ref[r] = turned[0:16].astype(bf16)
        grad_ref[r] = turned[16:32].astype(bf16)


def finish_kernel(one_ref, other_ref, grad_ref):
    total = one_ref[...] + other_ref[...]
    for tap in range(27):
        slot = tap % 14
        block = total[16 * slot : 16 * slot + 16]
        grad_ref[tap] = block[:, 0:64] if tap < 14 else block[:, 64:128]


def body(features, weight, cotangent, neighbours):
    bricks, narrow = features.shape[0], features.shape[1]
    rows = bricks * narrow
    length = lax.axis_size("space")
    shape = jax.ShapeDtypeStruct

    def across(name, value, apart, axis="chan"):
        with jax.named_scope(name):
            return lax.ppermute(value, axis, [(i, i ^ apart) for i in range(lax.axis_size(axis))])

    inputs = (features, cotangent, weight, neighbours)
    inputs = (features, cotangent, weight, neighbours)
    both, own, near, first, second = call(
        prepare_kernel,
        (
            shape((bricks, narrow, 1024), bf16),
            shape(weight.shape, bf16),
            shape(neighbours.shape, i32),
            shape((rows, 128), bf16),
            shape((rows, 128), bf16),
        ),
        [pltpu.SemaphoreType.DMA((4,))],
        *(pltpu.with_memory_space_constraint(view, pltpu.HBM) for view in inputs),
        specs=[HBM] * 4,
    )
    def meet(value, begin):
        mates = {i: i + 1 for i in range(begin, length - 1, 2)}
        mates.update({after: before for before, after in mates.items()})
        wide = lax.axis_size("chan")
        place = lambda i, c: mates[i] * wide + c if i in mates else i * wide + (c ^ 1)
        pairs = [(i * wide + c, place(i, c)) for i in range(length) for c in range(wide)]
        return lax.ppermute(value, ("space", "chan"), pairs)

    with jax.named_scope("plane_first"):
        first = meet(first, 0)
    with jax.named_scope("plane_second"):
        second = meet(second, 1)
    both1 = across("both_core", both, 1)
    feat2 = across("feat_y", features, 2)
    windows, sums = call(
        near_grad_kernel,
        (shape((14, 512, 256), bf16), shape((4, 32, 128), f32)),
        [pltpu.VMEM((3, 10, 10, 8, 128), f32), pltpu.VMEM((28, 2 * rows, 128), f32)],
        near, both, both1,
        specs=[VMEM] * 3,
    )
    first, second, sums = lax.optimization_barrier((first, second, sums))
    near_pack, far_pack = call(
        pack_kernel,
        (shape((rows, 384), bf16), shape((rows, 896), bf16)),
        [],
        both, own, first, second,
        specs=[VMEM] * 4,
    )
    far_pack2 = across("pack_y", far_pack, 2)
    edge_windows, sums = call(
        halo_grad_kernel,
        (shape((2, 64, 1152), bf16), shape((4, 32, 128), f32)),
        [pltpu.VMEM((2, 3, 10, 8, 128), f32), pltpu.VMEM((27, 2 * rows, 128), f32)],
        near, near_pack, both, both1, sums,
        specs=[VMEM] * 5,
    )
    feat3 = across("feat_far", feat2, 1)
    part = call(
        functools.partial(far_grad_kernel, float(bricks * length * 512) ** -0.5),
        shape((224, 128), f32),
        [pltpu.VMEM((27, 2 * rows, 128), f32), pltpu.VMEM((4, 64, 128), f32)],
        windows, edge_windows, feat2, feat3, sums,
        specs=[VMEM] * 5,
    )
    steps = []
    step = 1
    while step < length:
        steps.append(step)
        step *= 2
    other = across("sum_first", part, steps[0], "space")
    near_pack1 = across("pack_core", near_pack, 1)
    far_pack3 = across("pack_far", far_pack2, 1)
    grid, matrix = call(
        inner_kernel,
        (shape((6400, 128), bf16), shape((1152, 128), bf16)),
        [
            pltpu.VMEM(((bricks + 1) * 512, 128), f32),
            pltpu.VMEM((6400, 128), f32),
            pltpu.SMEM(neighbours.shape, i32),
            pltpu.SemaphoreType.DMA,
        ],
        near, own, both, both1, feat2, feat3, near_pack, near_pack1, far_pack2, far_pack3,
        specs=[VMEM] * 10,
    )
    for step in steps[1:]:
        part = part + other
        if step < steps[-1]:
            other = across("sum_next", part, step, "space")
            other, grid = lax.optimization_barrier((other, grid))
        else:
            other = across("sum_last", part, step, "space")
    middle = call(middle_kernel, shape((3072, 128), f32), [], grid, matrix, specs=[VMEM, VMEM])
    output, grad_input = call(
        outer_kernel,
        (shape(features.shape, bf16), shape(features.shape, bf16)),
        [
            pltpu.VMEM(((bricks + 1) * 128, 128), f32),
            pltpu.VMEM((1600, 128), f32),
            pltpu.VMEM((1600, 128), bf16),
            pltpu.VMEM((512, 128), f32),
            pltpu.VMEM((512, 128), f32),
            pltpu.SMEM(neighbours.shape, i32),
            pltpu.SemaphoreType.DMA,
        ],
        near, grid, matrix, middle, near_pack, near_pack1, far_pack2, far_pack3,
        specs=[VMEM] * 8,
    )
    other, output, grad_input = lax.optimization_barrier((other, output, grad_input))
    grad_weight = call(finish_kernel, shape(weight.shape, f32), [], part, other, specs=[VMEM, VMEM])
    return (output, grad_input, grad_weight)


def solution(mesh):
    in_specs = (
        P("space", "chan", None),
        P(None, "chan", None),
        P("space", "chan", None),
        P("space", None),
    )
    out_specs = (P("space", "chan", None), P("space", "chan", None), P(None, "chan", None))
    return jax.shard_map(body, mesh=mesh, in_specs=in_specs, out_specs=out_specs, check_vma=False)
```

```python
import functools

import jax
import jax.numpy as jnp
from jax import lax
from jax.experimental import pallas as pl
from jax.experimental.pallas import tpu as pltpu
from jax.sharding import PartitionSpec as P

f32, bf16, i32 = jnp.float32, jnp.bfloat16, jnp.int32
VMEM = pl.BlockSpec(memory_space=pltpu.VMEM)
HBM = pl.BlockSpec(memory_space=pltpu.HBM)

COSTS = {"pack_kernel": 2_000_000_000}
GROUPS = ((0, 8), (8, 14), (14, 22), (22, 27))


def iota(shape, axis):
    return lax.broadcasted_iota(i32, shape, axis)


def call(kernel, out_shape, scratch, *args, specs, out_spec=VMEM):
    name = getattr(kernel, "func", kernel).__name__
    return pl.pallas_call(
        kernel,
        name=name,
        out_shape=out_shape,
        in_specs=specs,
        out_specs=jax.tree.map(lambda _: out_spec, out_shape),
        scratch_shapes=scratch,
        compiler_params=pltpu.CompilerParams(vmem_limit_bytes=48 << 20),
        cost_estimate=pl.CostEstimate(flops=COSTS.get(name, 0), bytes_accessed=0, transcendentals=0),
    )(*args)


def prepare_kernel(feat_any, cot_any, weight_any, near_any, both_ref, weight_ref, near_ref, first_ref, second_ref, sems):
    rows = first_ref.shape[0]
    pairs = (
        (feat_any, both_ref.at[:, :, 0:512]),
        (cot_any, both_ref.at[:, :, 512:1024]),
        (weight_any, weight_ref),
        (near_any, near_ref),
    )
    copies = [pltpu.make_async_copy(source, target, sems.at[i]) for i, (source, target) in enumerate(pairs)]
    for copy in copies:
        copy.start()
    for copy in copies[:2]:
        copy.wait()
    low = jnp.concatenate([both_ref[:, :, i : i + 64].reshape(rows, 64) for i in (0, 512)], axis=1)
    high = jnp.concatenate([both_ref[:, :, i : i + 64].reshape(rows, 64) for i in (448, 960)], axis=1)
    even = lax.axis_index("space") % 2 == 0

    @pl.when(even)
    def _():
        first_ref[...] = high
        second_ref[...] = low

    @pl.when(jnp.logical_not(even))
    def _():
        first_ref[...] = low
        second_ref[...] = high

    for copy in copies[2:]:
        copy.wait()


def pack_kernel(second_ref, first_ref, weight_ref, near_pack_ref, far_pack_ref):
    rows = first_ref.shape[0]
    even = jnp.full((rows, 128), lax.axis_index("space") % 2, i32) == 0
    first, second = first_ref[...].astype(f32), second_ref[...].astype(f32)
    before = jnp.where(even, second, first)
    after = jnp.where(even, first, second)
    left = iota((rows, 128), 1) < 64
    feat = jnp.where(left, before, pltpu.roll(after, 64, 1)).astype(bf16)
    cot = jnp.where(left, pltpu.roll(before, 64, 1), after).astype(bf16)
    groups = []
    for group in range(4):
        taps = [weight_ref[8 * group + t] if 8 * group + t < 27 else jnp.zeros((16, 64), bf16) for t in range(8)]
        groups.append(jnp.concatenate(taps, axis=0))
    kernel = jnp.concatenate(groups, axis=1)
    spots, lanes = iota((256, 128), 0), iota((256, 128), 1)
    place = lax.axis_index("chan") // 2
    for target, pair in ((near_pack_ref, place), (far_pack_ref, place ^ 1)):
        target[:, 0:128] = feat
        target[:, 128:256] = cot
        owned = spots == 64 * (lanes // 32) + 32 * pair + lanes % 32
        part = jnp.dot(kernel, owned.astype(f32).astype(bf16), preferred_element_type=f32)
        target[:, 256:384] = part.astype(bf16)


def tap_sums(products, count, bricks):
    lane_group = iota((16, 128), 1) // 16
    sums = []
    for begin, end in GROUPS:
        blocks = []
        for view in range(count):
            total = None
            for shift in range(8):
                chosen = None
                for brick in range(bricks):
                    start = (view * bricks + brick) * 16
                    block = products[min(begin + (brick + shift) % 8, end - 1), start : start + 16, :]
                    chosen = block if chosen is None else jnp.where(lane_group == brick, block, chosen)
                if shift:
                    chosen = pltpu.roll(chosen, 16 * shift, 1)
                total = chosen if total is None else total + chosen
            blocks.append(total)
        sums.append(blocks)
    return sums


def brick_picker(near_ref, rows):
    bricks = near_ref.shape[0]
    listed = near_ref[...]
    listed = jnp.where(listed < 0, bricks, listed % bricks).astype(f32)
    widen = (iota((bricks, rows), 1) // 16 == iota((bricks, rows), 0)).astype(f32)
    source = lax.dot_general(listed, widen, (((0,), (0,)), ((), ())), preferred_element_type=f32)
    source = source.astype(i32) * 16 + iota((27, rows), 1) % 16
    row_ids = iota((rows, rows), 0)

    def pick(i, j):
        first = 9 * i + 3 * j
        picks = [(row_ids == source[first + k : first + k + 1, :]).astype(f32).astype(bf16) for k in range(3)]
        return jnp.concatenate(picks, axis=1)

    return pick


def shifted_columns(columns, pick, j):
    if j != 1:
        columns = columns[:, 7:8] if j == 0 else columns[:, 0:1]
    wide, deep = columns.shape[0], columns.shape[1]
    count = wide * deep
    edge = iota((1, 8, 128), 1)
    moved = jnp.dot(columns.reshape(count * 8, 128), pick, preferred_element_type=f32)
    lower, own, upper = (moved[:, 128 * k : 128 * k + 128].reshape(count, 8, 128) for k in range(3))
    down = jnp.where(edge == 0, pltpu.roll(lower, 1, 1), pltpu.roll(own, 1, 1))
    up = jnp.where(edge == 7, pltpu.roll(upper, 7, 1), pltpu.roll(own, 7, 1))
    return [value.reshape(wide, deep, 8, 128) for value in (down, own, up)]


ROWS_TO = ((0, 1), (1, 9), (9, 10))


def near_grad_kernel(near_ref, both_ref, both1_ref, windows_ref, sums_ref, padded, products):
    bricks = near_ref.shape[0]
    rows = bricks * 16
    flat = jnp.transpose(both_ref[:, :, 512:1024].reshape(rows, 512).astype(f32)).astype(bf16).reshape(8, 8, 8, 128)
    pick = brick_picker(near_ref, rows)
    for x in (0, 9):
        padded[:, x] = jnp.zeros((3, 10, 8, 128), f32)
    for j in range(3):
        for c, value in enumerate(shifted_columns(flat, pick(1, j), j)):
            padded[c, 1:9, ROWS_TO[j][0] : ROWS_TO[j][1]] = value
    feat = jnp.concatenate([view[:, :, 0:512].reshape(rows, 512) for view in (both_ref, both1_ref)], axis=0)
    for pair in range(14):
        views = []
        for tap in (2 * pair, min(2 * pair + 1, 26)):
            a, b, c = (26 - tap) // 9, (26 - tap) // 3 % 3, (26 - tap) % 3
            views.append(padded[c, a : a + 8, b : b + 8].reshape(512, 128).astype(bf16))
        window = jnp.concatenate(views, axis=1)
        windows_ref[pair] = window
        both = jnp.dot(feat, window, preferred_element_type=f32)
        products[2 * pair] = both[:, 0:128]
        products[2 * pair + 1] = both[:, 128:256]
    sums = tap_sums(products, 2, bricks)
    for group in range(4):
        sums_ref[group] = jnp.concatenate(sums[group], axis=0)


def plane_ends(views, side):
    rows = views[0].shape[0] * 16
    start = 0 if side == 0 else 448
    return jnp.concatenate([view[:, :, start : start + 64].reshape(rows, 64) for view in views], axis=0)


def halo_grad_kernel(near_ref, packed_ref, both_ref, both1_ref, sums_ref, windows_ref, total_ref, edges, products):
    bricks = near_ref.shape[0]
    rows = bricks * 16
    planes = jnp.transpose(packed_ref[:, 128:256].astype(f32)).astype(bf16)
    pick = brick_picker(near_ref, rows)
    for side in range(2):
        columns = planes[64 * side : 64 * side + 64].reshape(1, 8, 8, 128)
        for j in range(3):
            for c, value in enumerate(shifted_columns(columns, pick(2 * side, j), j)):
                edges[side, c, ROWS_TO[j][0] : ROWS_TO[j][1]] = value.reshape(value.shape[1:])
    for side in range(2):
        views = []
        for place in range(9):
            b, c = (8 - place) // 3, (8 - place) % 3
            views.append(edges[side, c, b : b + 8].reshape(64, 128).astype(bf16))
        window = jnp.concatenate(views, axis=1)
        windows_ref[side] = window
        both = jnp.dot(plane_ends([both_ref, both1_ref], side), window, preferred_element_type=f32)
        for place in range(9):
            products[18 * (1 - side) + place] = both[:, 128 * place : 128 * place + 128]
    for place in range(9, 18):
        products[place] = jnp.zeros((2 * rows, 128), f32)
    sums = tap_sums(products, 2, bricks)
    for group in range(4):
        total_ref[group] = sums_ref[group] + jnp.concatenate(sums[group], axis=0)


def far_grad_kernel(scale, windows_ref, edge_windows_ref, feat2_ref, feat3_ref, sums_ref, part_ref, products, ordered):
    chan = lax.axis_index("chan")
    bricks = feat2_ref.shape[0]
    rows = bricks * 16
    views = [feat2_ref, feat3_ref]
    for side in range(2):
        both = jnp.dot(plane_ends(views, side), edge_windows_ref[side], preferred_element_type=f32)
        for place in range(9):
            products[18 * (1 - side) + place] = both[:, 128 * place : 128 * place + 128]
    far = jnp.concatenate([view[...].reshape(rows, 512) for view in views], axis=0)
    for pair in range(14):
        both = jnp.dot(far, windows_ref[pair], preferred_element_type=f32)
        for tap in range(2 * pair, min(2 * pair + 2, 27)):
            one = both[:, 128 * (tap % 2) : 128 * (tap % 2) + 128]
            products[tap] = one if 9 <= tap < 18 else one + products[tap]
    sums = tap_sums(products, 2, bricks)
    for group in range(4):
        both = sums_ref[group]
        for apart, block in enumerate((both[0:16], both[16:32], *sums[group])):
            ordered[group, pl.ds(pl.multiple_of(16 * (chan ^ apart), 16), 16), :] = block
    part_ref[0:128] = jnp.transpose(jnp.concatenate([ordered[0], ordered[2]], axis=0)) * scale
    part_ref[128:224] = jnp.transpose(jnp.concatenate([ordered[1], ordered[3]], axis=0))[0:96] * scale


def pad_bricks(near, padded, source, size, xs):
    bricks = near.shape[0]
    for r in range(bricks):
        for i, base, x_pairs in xs:
            for j in range(3):
                for k in range(3):
                    listed = near[r, 9 * i + 3 * j + k]
                    start = jnp.where(listed < 0, bricks, listed % bricks) * size + base
                    y_pairs = [(y + 1, y) for y in range(8)] if j == 1 else [(0, 7) if j == 0 else (9, 0)]
                    z_to, z_from = (1, 0) if k == 1 else ((0, 7) if k == 0 else (9, 0))
                    if k == 1:
                        for x_to, x_from in x_pairs:
                            for y_to, y_from in y_pairs:
                                piece = source[pl.ds(start + 64 * x_from + 8 * y_from, 8), :]
                                padded[pl.ds(80 * (10 * x_to + y_to) + 8 + r, 8, 8), :] = piece
                    elif j == 1:
                        for x_to, x_from in x_pairs:
                            piece = source[pl.ds(start + 64 * x_from + z_from, 8, 8), :]
                            padded[pl.ds(80 * (10 * x_to + 1) + 8 * z_to + r, 8, 80), :] = piece
                    elif i == 1:
                        piece = source[pl.ds(start + 8 * y_pairs[0][1] + z_from, 8, 64), :]
                        padded[pl.ds(80 * y_pairs[0][0] + 8 * z_to + r, 8, 800), :] = piece
                    else:
                        piece = source[pl.ds(start + 8 * y_pairs[0][1] + z_from, 1), :]
                        padded[pl.ds(80 * (10 * x_pairs[0][0] + y_pairs[0][0]) + 8 * z_to + r, 1), :] = piece


def inner_kernel(near_ref, *refs):
    (both, both1), feats, cots, (grid_ref, flat, padded, near, sem) = refs[:2], refs[2:4], refs[4:6], refs[6:]
    copy = pltpu.make_async_copy(near_ref, near, sem)
    copy.start()
    bricks = near_ref.shape[0]
    feats = [both.at[:, :, 0:512], both1.at[:, :, 0:512], *feats]
    cots = [both.at[:, :, 512:1024], both1.at[:, :, 512:1024], *cots]
    for s in range(bricks):
        pair = jnp.concatenate([view[s] for view in feats + cots], axis=0)
        flat[512 * s : 512 * s + 512] = jnp.transpose(pair.astype(f32))
    flat[512 * bricks : 512 * bricks + 512] = jnp.zeros((512, 128), f32)
    copy.wait()
    pad_bricks(near, padded, flat, 512, [(1, 0, [(x, x) for x in range(8)])])
    for x in range(8):
        grid_ref[800 * x : 800 * x + 800] = padded[800 * x : 800 * x + 800].astype(bf16)


def matrix_kernel(weight_ref, *refs):
    packs, mat_ref = refs[:4], refs[4]
    chan = lax.axis_index("chan")
    lanes = iota((48, 128), 1)
    spots = iota((48, 128), 0)
    forward = (lanes == 32 * (spots // 16) + spots % 16).astype(f32).astype(bf16)
    lanes = iota((128, 128), 1)
    spots = iota((128, 128), 0)
    picks = {}
    for group in range(4):
        for c in range(3):
            hit = lanes - 32 * c - 16 == spots - 32 * group - 16 * (chan % 2)
            hit = hit & (lanes >= 32 * c + 16) & (lanes < 32 * c + 32)
            picks[group, c] = hit.astype(f32).astype(bf16)
    for spot in range(9):
        own = weight_ref[3 * spot : 3 * spot + 3].reshape(48, 64)
        turned = lax.dot_general(own, forward, (((0,), (0,)), ((), ())), preferred_element_type=f32).astype(bf16)
        for q in range(4):
            mat_ref[pl.ds(pl.multiple_of(128 * spot + 16 * (chan ^ q), 16), 16), :] = turned[16 * q : 16 * q + 16]
        total = None
        for c in range(3):
            tap = 26 - 3 * spot - c
            block = jnp.concatenate([pack[16 * (tap % 8) : 16 * (tap % 8) + 16, 256:384] for pack in packs], axis=0)
            term = jnp.dot(block, picks[tap // 8, c], preferred_element_type=f32)
            total = term if total is None else total + term
        mat_ref[128 * spot + 64 : 128 * spot + 128] = total.astype(bf16)


def conv_layer(views, mat_ref):
    pieces = [view[80 * b : 80 * b + 640, :] for view in views for b in range(3)]
    sums = jnp.dot(jnp.concatenate(pieces, axis=1), mat_ref[...], preferred_element_type=f32).reshape(8, 80, 128)
    total = sums[:, 0:64] + pltpu.roll(sums[:, 8:72], 96, 2) + pltpu.roll(sums[:, 16:80], 64, 2)
    return total.reshape(512, 128)


def middle_kernel(grid_ref, mat_ref, done_ref):
    for x in range(6):
        views = [grid_ref.at[800 * (x + a) : 800 * (x + a) + 800] for a in range(3)]
        done_ref[512 * x : 512 * x + 512] = conv_layer(views, mat_ref)


def outer_kernel(near_ref, grid_ref, mat_ref, middle_ref, *refs):
    packs, (out_any, grad_any, out, grad, planes, padded, edges, low, high, near, sem, sems) = refs[:4], refs[4:]
    copy = pltpu.make_async_copy(near_ref, near, sem)
    copy.start()
    bricks = near_ref.shape[0]
    for s in range(bricks):
        rows = slice(16 * s, 16 * s + 16)
        pair = jnp.concatenate([pack[rows, 0:128] for pack in packs] + [pack[rows, 128:256] for pack in packs], axis=0)
        planes[128 * s : 128 * s + 128] = jnp.transpose(pair.astype(f32))
    planes[128 * bricks : 128 * bricks + 128] = jnp.zeros((128, 128), f32)
    copy.wait()
    pad_bricks(near, padded, planes, 128, [(0, 0, [(0, 0)]), (2, 64, [(1, 0)])])
    edges[...] = padded[...].astype(bf16)
    layers = [edges.at[0:800]] + [grid_ref.at[800 * x : 800 * x + 800] for x in (0, 1, 6, 7)] + [edges.at[800:1600]]
    low[...] = conv_layer(layers[0:3], mat_ref)
    high[...] = conv_layer(layers[3:6], mat_ref)
    for r in range(bricks):
        views = [low[pl.ds(r, 64, 8), :], middle_ref[pl.ds(r, 384, 8), :], high[pl.ds(r, 64, 8), :]]
        turned = jnp.transpose(jnp.concatenate(views, axis=0))
        out[r] = turned[0:16].astype(bf16)
        grad[r] = turned[16:32].astype(bf16)
        pltpu.make_async_copy(out.at[r], out_any.at[r], sems.at[0, r]).start()
        pltpu.make_async_copy(grad.at[r], grad_any.at[r], sems.at[1, r]).start()
    for r in range(bricks):
        pltpu.make_async_copy(out.at[r], out_any.at[r], sems.at[0, r]).wait()
        pltpu.make_async_copy(grad.at[r], grad_any.at[r], sems.at[1, r]).wait()


def finish_kernel(one_ref, other_ref, grad_ref):
    total = one_ref[...] + other_ref[...]
    for tap in range(27):
        slot = tap % 14
        block = total[16 * slot : 16 * slot + 16]
        grad_ref[tap] = block[:, 0:64] if tap < 14 else block[:, 64:128]


def body(features, weight, cotangent, neighbours):
    bricks, narrow = features.shape[0], features.shape[1]
    rows = bricks * narrow
    length = lax.axis_size("space")
    shape = jax.ShapeDtypeStruct

    def across(name, value, apart, axis="chan"):
        with jax.named_scope(name):
            return lax.ppermute(value, axis, [(i, i ^ apart) for i in range(lax.axis_size(axis))])

    inputs = (features, cotangent, weight, neighbours)
    inputs = (features, cotangent, weight, neighbours)
    both, own, near, first, second = call(
        prepare_kernel,
        (
            shape((bricks, narrow, 1024), bf16),
            shape(weight.shape, bf16),
            shape(neighbours.shape, i32),
            shape((rows, 128), bf16),
            shape((rows, 128), bf16),
        ),
        [pltpu.SemaphoreType.DMA((4,))],
        *(pltpu.with_memory_space_constraint(view, pltpu.HBM) for view in inputs),
        specs=[HBM] * 4,
    )
    def meet(value, begin):
        mates = {i: i + 1 for i in range(begin, length - 1, 2)}
        mates.update({after: before for before, after in mates.items()})
        wide = lax.axis_size("chan")
        place = lambda i, c: mates[i] * wide + c if i in mates else i * wide + (c ^ 1)
        pairs = [(i * wide + c, place(i, c)) for i in range(length) for c in range(wide)]
        return lax.ppermute(value, ("space", "chan"), pairs)

    with jax.named_scope("plane_second"):
        second = meet(second, 1)
    with jax.named_scope("plane_first"):
        first = meet(first, 0)
    both1 = across("both_core", both, 1)
    feat2 = across("feat_y", features, 2)
    cot2 = across("cot_y", cotangent, 2)
    windows, sums = call(
        near_grad_kernel,
        (shape((14, 512, 256), bf16), shape((4, 32, 128), f32)),
        [pltpu.VMEM((3, 10, 10, 8, 128), f32), pltpu.VMEM((28, 2 * rows, 128), f32)],
        near, both, both1,
        specs=[VMEM] * 3,
    )
    second, first, sums = lax.optimization_barrier((second, first, sums))
    near_pack, far_pack = call(
        pack_kernel,
        (shape((rows, 384), bf16), shape((rows, 384), bf16)),
        [],
        second, first, own,
        specs=[VMEM] * 3,
    )
    feat2, windows = lax.optimization_barrier((feat2, windows))
    feat3 = across("feat_far", feat2, 1)
    edge_windows, sums = call(
        halo_grad_kernel,
        (shape((2, 64, 1152), bf16), shape((4, 32, 128), f32)),
        [pltpu.VMEM((2, 3, 10, 8, 128), f32), pltpu.VMEM((27, 2 * rows, 128), f32)],
        near, near_pack, both, both1, sums,
        specs=[VMEM] * 5,
    )
    part = call(
        functools.partial(far_grad_kernel, float(bricks * length * 512) ** -0.5),
        shape((224, 128), f32),
        [pltpu.VMEM((27, 2 * rows, 128), f32), pltpu.VMEM((4, 64, 128), f32)],
        windows, edge_windows, feat2, feat3, sums,
        specs=[VMEM] * 5,
    )
    steps = []
    step = 1
    while step < length:
        steps.append(step)
        step *= 2
    other = across("sum_first", part, steps[0], "space")
    cot2, far_pack, part = lax.optimization_barrier((cot2, far_pack, part))
    cot3 = across("cot_far", cot2, 1)
    far_pack2 = across("pack_y", far_pack, 2)
    near_pack1 = across("pack_core", near_pack, 1)
    far_pack3 = across("pack_far", far_pack2, 1)
    grid = call(
        inner_kernel,
        shape((6400, 128), bf16),
        [
            pltpu.VMEM(((bricks + 1) * 512, 128), f32),
            pltpu.VMEM((6400, 128), f32),
            pltpu.SMEM(neighbours.shape, i32),
            pltpu.SemaphoreType.DMA,
        ],
        near, both, both1, feat2, feat3, cot2, cot3,
        specs=[VMEM] * 7,
    )
    other, grid = lax.optimization_barrier((other, grid))
    matrix = call(
        matrix_kernel,
        shape((1152, 128), bf16),
        [],
        own, near_pack, near_pack1, far_pack2, far_pack3,
        specs=[VMEM] * 5,
    )
    for step in steps[1:]:
        part = part + other
        if step < steps[-1]:
            other = across("sum_next", part, step, "space")
            other, matrix = lax.optimization_barrier((other, matrix))
        else:
            other = across("sum_last", part, step, "space")
    middle = call(middle_kernel, shape((3072, 128), f32), [], grid, matrix, specs=[VMEM, VMEM])
    output, grad_input = call(
        outer_kernel,
        (shape(features.shape, bf16), shape(features.shape, bf16)),
        [
            pltpu.VMEM(features.shape, bf16),
            pltpu.VMEM(features.shape, bf16),
            pltpu.VMEM(((bricks + 1) * 128, 128), f32),
            pltpu.VMEM((1600, 128), f32),
            pltpu.VMEM((1600, 128), bf16),
            pltpu.VMEM((512, 128), f32),
            pltpu.VMEM((512, 128), f32),
            pltpu.SMEM(neighbours.shape, i32),
            pltpu.SemaphoreType.DMA,
            pltpu.SemaphoreType.DMA((2, bricks)),
        ],
        near, grid, matrix, middle, near_pack, near_pack1, far_pack2, far_pack3,
        specs=[VMEM] * 8,
        out_spec=HBM,
    )
    other, output, grad_input = lax.optimization_barrier((other, output, grad_input))
    grad_weight = call(finish_kernel, shape(weight.shape, f32), [], part, other, specs=[VMEM, VMEM])
    return (output, grad_input, grad_weight)


def solution(mesh):
    in_specs = (
        P("space", "chan", None),
        P(None, "chan", None),
        P("space", "chan", None),
        P("space", None),
    )
    out_specs = (P("space", "chan", None), P("space", "chan", None), P(None, "chan", None))
    return jax.shard_map(body, mesh=mesh, in_specs=in_specs, out_specs=out_specs, check_vma=False)
```

```python
import functools

import jax
import jax.numpy as jnp
from jax import lax
from jax.experimental import pallas as pl
from jax.experimental.pallas import tpu as pltpu
from jax.sharding import PartitionSpec as P

f32, bf16, i32 = jnp.float32, jnp.bfloat16, jnp.int32
VMEM = pl.BlockSpec(memory_space=pltpu.VMEM)
HBM = pl.BlockSpec(memory_space=pltpu.HBM)

COSTS = {"pack_kernel": 2_000_000_000}
EARLY = 1
GROUPS = ((0, 8), (8, 14), (14, 22), (22, 27))


def iota(shape, axis):
    return lax.broadcasted_iota(i32, shape, axis)


def call(kernel, out_shape, scratch, *args, specs, out_spec=VMEM):
    name = getattr(kernel, "func", kernel).__name__
    return pl.pallas_call(
        kernel,
        name=name,
        out_shape=out_shape,
        in_specs=specs,
        out_specs=jax.tree.map(lambda _: out_spec, out_shape),
        scratch_shapes=scratch,
        compiler_params=pltpu.CompilerParams(vmem_limit_bytes=48 << 20),
        cost_estimate=pl.CostEstimate(flops=COSTS.get(name, 0), bytes_accessed=0, transcendentals=0),
    )(*args)


def prepare_kernel(feat_any, cot_any, weight_any, near_any, both_ref, weight_ref, near_ref, first_ref, second_ref, sems):
    rows = first_ref.shape[0]
    pairs = (
        (feat_any, both_ref.at[:, :, 0:512]),
        (cot_any, both_ref.at[:, :, 512:1024]),
        (weight_any, weight_ref),
        (near_any, near_ref),
    )
    copies = [pltpu.make_async_copy(source, target, sems.at[i]) for i, (source, target) in enumerate(pairs)]
    for copy in copies:
        copy.start()
    for copy in copies[:2]:
        copy.wait()
    low = jnp.concatenate([both_ref[:, :, i : i + 64].reshape(rows, 64) for i in (0, 512)], axis=1)
    high = jnp.concatenate([both_ref[:, :, i : i + 64].reshape(rows, 64) for i in (448, 960)], axis=1)
    even = lax.axis_index("space") % 2 == 0

    @pl.when(even)
    def _():
        first_ref[...] = high
        second_ref[...] = low

    @pl.when(jnp.logical_not(even))
    def _():
        first_ref[...] = low
        second_ref[...] = high

    for copy in copies[2:]:
        copy.wait()


def pack_kernel(second_ref, first_ref, weight_ref, near_pack_ref, far_pack_ref):
    rows = first_ref.shape[0]
    even = jnp.full((rows, 128), lax.axis_index("space") % 2, i32) == 0
    first, second = first_ref[...].astype(f32), second_ref[...].astype(f32)
    before = jnp.where(even, second, first)
    after = jnp.where(even, first, second)
    left = iota((rows, 128), 1) < 64
    feat = jnp.where(left, before, pltpu.roll(after, 64, 1)).astype(bf16)
    cot = jnp.where(left, pltpu.roll(before, 64, 1), after).astype(bf16)
    groups = []
    for group in range(4):
        taps = [weight_ref[8 * group + t] if 8 * group + t < 27 else jnp.zeros((16, 64), bf16) for t in range(8)]
        groups.append(jnp.concatenate(taps, axis=0))
    kernel = jnp.concatenate(groups, axis=1)
    spots, lanes = iota((256, 128), 0), iota((256, 128), 1)
    place = lax.axis_index("chan") // 2
    for target, pair in ((near_pack_ref, place), (far_pack_ref, place ^ 1)):
        target[:, 0:128] = feat
        target[:, 128:256] = cot
        owned = spots == 64 * (lanes // 32) + 32 * pair + lanes % 32
        part = jnp.dot(kernel, owned.astype(f32).astype(bf16), preferred_element_type=f32)
        target[:, 256:384] = part.astype(bf16)


def tap_sums(products, count, bricks, absent=()):
    lane_group = iota((16, 128), 1) // 16
    sums = []
    for begin, end in GROUPS:
        blocks = []
        for view in range(count):
            total = None
            for shift in range(8):
                chosen = None
                for brick in range(bricks):
                    start = (view * bricks + brick) * 16
                    tap = min(begin + (brick + shift) % 8, end - 1)
                    block = jnp.zeros((16, 128), f32) if tap in absent else products[tap, start : start + 16, :]
                    chosen = block if chosen is None else jnp.where(lane_group == brick, block, chosen)
                if shift:
                    chosen = pltpu.roll(chosen, 16 * shift, 1)
                total = chosen if total is None else total + chosen
            blocks.append(total)
        sums.append(blocks)
    return sums


def brick_picker(near_ref, rows):
    bricks = near_ref.shape[0]
    listed = near_ref[...]
    listed = jnp.where(listed < 0, bricks, listed % bricks).astype(f32)
    widen = (iota((bricks, rows), 1) // 16 == iota((bricks, rows), 0)).astype(f32)
    source = lax.dot_general(listed, widen, (((0,), (0,)), ((), ())), preferred_element_type=f32)
    source = source.astype(i32) * 16 + iota((27, rows), 1) % 16
    row_ids = iota((rows, rows), 0)

    def pick(i, j):
        first = 9 * i + 3 * j
        picks = [(row_ids == source[first + k : first + k + 1, :]).astype(f32).astype(bf16) for k in range(3)]
        return jnp.concatenate(picks, axis=1)

    return pick


def shifted_columns(columns, pick, j):
    if j != 1:
        columns = columns[:, 7:8] if j == 0 else columns[:, 0:1]
    wide, deep = columns.shape[0], columns.shape[1]
    count = wide * deep
    edge = iota((1, 8, 128), 1)
    moved = jnp.dot(columns.reshape(count * 8, 128), pick, preferred_element_type=f32)
    lower, own, upper = (moved[:, 128 * k : 128 * k + 128].reshape(count, 8, 128) for k in range(3))
    down = jnp.where(edge == 0, pltpu.roll(lower, 1, 1), pltpu.roll(own, 1, 1))
    up = jnp.where(edge == 7, pltpu.roll(upper, 7, 1), pltpu.roll(own, 7, 1))
    return [value.reshape(wide, deep, 8, 128) for value in (down, own, up)]


ROWS_TO = ((0, 1), (1, 9), (9, 10))


def near_grad_kernel(near_ref, both_ref, both1_ref, windows_ref, sums_ref, padded, products):
    bricks = near_ref.shape[0]
    rows = bricks * 16
    flat = jnp.transpose(both_ref[:, :, 512:1024].reshape(rows, 512).astype(f32)).astype(bf16).reshape(8, 8, 8, 128)
    pick = brick_picker(near_ref, rows)
    for x in (0, 9):
        padded[:, x] = jnp.zeros((3, 10, 8, 128), f32)
    for j in range(3):
        for c, value in enumerate(shifted_columns(flat, pick(1, j), j)):
            padded[c, 1:9, ROWS_TO[j][0] : ROWS_TO[j][1]] = value
    feat = jnp.concatenate([view[:, :, 0:512].reshape(rows, 512) for view in (both_ref, both1_ref)], axis=0)
    for pair in range(14):
        views = []
        for tap in (2 * pair, min(2 * pair + 1, 26)):
            a, b, c = (26 - tap) // 9, (26 - tap) // 3 % 3, (26 - tap) % 3
            views.append(padded[c, a : a + 8, b : b + 8].reshape(512, 128).astype(bf16))
        window = jnp.concatenate(views, axis=1)
        windows_ref[pair] = window
        both = jnp.dot(feat, window, preferred_element_type=f32)
        products[2 * pair] = both[:, 0:128]
        products[2 * pair + 1] = both[:, 128:256]
    sums = tap_sums(products, 2, bricks)
    for group in range(4):
        sums_ref[group] = jnp.concatenate(sums[group], axis=0)


def plane_ends(views, side):
    rows = views[0].shape[0] * 16
    start = 0 if side == 0 else 448
    return jnp.concatenate([view[:, :, start : start + 64].reshape(rows, 64) for view in views], axis=0)


def halo_grad_kernel(near_ref, packed_ref, both_ref, both1_ref, sums_ref, windows_ref, total_ref, edges, products):
    bricks = near_ref.shape[0]
    rows = bricks * 16
    planes = jnp.transpose(packed_ref[:, 128:256].astype(f32)).astype(bf16)
    pick = brick_picker(near_ref, rows)
    for side in range(2):
        columns = planes[64 * side : 64 * side + 64].reshape(1, 8, 8, 128)
        for j in range(3):
            for c, value in enumerate(shifted_columns(columns, pick(2 * side, j), j)):
                edges[side, c, ROWS_TO[j][0] : ROWS_TO[j][1]] = value.reshape(value.shape[1:])
    for side in range(2):
        views = []
        for place in range(9):
            b, c = (8 - place) // 3, (8 - place) % 3
            views.append(edges[side, c, b : b + 8].reshape(64, 128).astype(bf16))
        window = jnp.concatenate(views, axis=1)
        windows_ref[side] = window
        both = jnp.dot(plane_ends([both_ref, both1_ref], side), window, preferred_element_type=f32)
        for place in range(9):
            products[18 * (1 - side) + place] = both[:, 128 * place : 128 * place + 128]
    sums = tap_sums(products, 2, bricks, range(9, 18))
    for group in range(4):
        total_ref[group] = sums_ref[group] + jnp.concatenate(sums[group], axis=0)


def far_grad_kernel(scale, windows_ref, edge_windows_ref, feat2_ref, feat3_ref, sums_ref, part_ref, products, ordered):
    chan = lax.axis_index("chan")
    bricks = feat2_ref.shape[0]
    rows = bricks * 16
    far = jnp.concatenate([view[...].reshape(rows, 512) for view in (feat2_ref, feat3_ref)], axis=0)
    for pair in range(14):
        halves = []
        for index, tap in enumerate((2 * pair, min(2 * pair + 1, 26))):
            half = windows_ref[pair, :, 128 * index : 128 * index + 128]
            edge = slice(128 * (tap % 9), 128 * (tap % 9) + 128)
            if tap < 9:
                half = jnp.concatenate([half[0:448], edge_windows_ref[1, :, edge]], axis=0)
            elif tap >= 18:
                half = jnp.concatenate([edge_windows_ref[0, :, edge], half[64:512]], axis=0)
            halves.append(half)
        both = jnp.dot(far, jnp.concatenate(halves, axis=1), preferred_element_type=f32)
        products[2 * pair] = both[:, 0:128]
        products[2 * pair + 1] = both[:, 128:256]
    sums = tap_sums(products, 2, bricks)
    for group in range(4):
        both = sums_ref[group]
        for apart, block in enumerate((both[0:16], both[16:32], *sums[group])):
            ordered[group, pl.ds(pl.multiple_of(16 * (chan ^ apart), 16), 16), :] = block
    turned = [jnp.transpose(jnp.concatenate([ordered[i], ordered[i + 2]], axis=0)) * scale for i in range(2)]
    turned = jnp.concatenate([turned[0], turned[1][0:96]], axis=0)
    upper = jnp.concatenate([pltpu.roll(turned[216:224], 64, 1), turned[0:208]], axis=0)
    part_ref[...] = jnp.where(iota((216, 128), 1) < 64, turned[0:216], upper)


def pad_bricks(near, padded, source, size, xs):
    bricks = near.shape[0]
    for r in range(bricks):
        for i, base, x_pairs in xs:
            for j in range(3):
                for k in range(3):
                    listed = near[r, 9 * i + 3 * j + k]
                    start = jnp.where(listed < 0, bricks, listed % bricks) * size + base
                    y_pairs = [(y + 1, y) for y in range(8)] if j == 1 else [(0, 7) if j == 0 else (9, 0)]
                    z_to, z_from = (1, 0) if k == 1 else ((0, 7) if k == 0 else (9, 0))
                    if k == 1:
                        for x_to, x_from in x_pairs:
                            for y_to, y_from in y_pairs:
                                piece = source[pl.ds(start + 64 * x_from + 8 * y_from, 8), :]
                                padded[pl.ds(80 * (10 * x_to + y_to) + 8 + r, 8, 8), :] = piece
                    elif j == 1:
                        for x_to, x_from in x_pairs:
                            piece = source[pl.ds(start + 64 * x_from + z_from, 8, 8), :]
                            padded[pl.ds(80 * (10 * x_to + 1) + 8 * z_to + r, 8, 80), :] = piece
                    elif i == 1:
                        piece = source[pl.ds(start + 8 * y_pairs[0][1] + z_from, 8, 64), :]
                        padded[pl.ds(80 * y_pairs[0][0] + 8 * z_to + r, 8, 800), :] = piece
                    else:
                        piece = source[pl.ds(start + 8 * y_pairs[0][1] + z_from, 1), :]
                        padded[pl.ds(80 * (10 * x_pairs[0][0] + y_pairs[0][0]) + 8 * z_to + r, 1), :] = piece


def inner_kernel(near_ref, *refs):
    (both, both1), feats, cots, (grid_ref, flat, padded, near, sem) = refs[:2], refs[2:4], refs[4:6], refs[6:]
    copy = pltpu.make_async_copy(near_ref, near, sem)
    copy.start()
    bricks = near_ref.shape[0]
    feats = [both.at[:, :, 0:512], both1.at[:, :, 0:512], *feats]
    cots = [both.at[:, :, 512:1024], both1.at[:, :, 512:1024], *cots]
    for s in range(bricks):
        pair = jnp.concatenate([view[s] for view in feats + cots], axis=0)
        flat[512 * s : 512 * s + 512] = jnp.transpose(pair.astype(f32))
    flat[512 * bricks : 512 * bricks + 512] = jnp.zeros((512, 128), f32)
    copy.wait()
    pad_bricks(near, padded, flat, 512, [(1, 0, [(x, x) for x in range(8)])])
    for x in range(8):
        grid_ref[800 * x : 800 * x + 800] = padded[800 * x : 800 * x + 800].astype(bf16)


def matrix_kernel(weight_ref, *refs):
    packs, mat_ref = refs[:4], refs[4]
    chan = lax.axis_index("chan")
    lanes = iota((48, 128), 1)
    spots = iota((48, 128), 0)
    forward = (lanes == 32 * (spots // 16) + spots % 16).astype(f32).astype(bf16)
    lanes = iota((128, 128), 1)
    spots = iota((128, 128), 0)
    picks = {}
    for group in range(4):
        for c in range(3):
            hit = lanes - 32 * c - 16 == spots - 32 * group - 16 * (chan % 2)
            hit = hit & (lanes >= 32 * c + 16) & (lanes < 32 * c + 32)
            picks[group, c] = hit.astype(f32).astype(bf16)
    for spot in range(9):
        own = weight_ref[3 * spot : 3 * spot + 3].reshape(48, 64)
        turned = lax.dot_general(own, forward, (((0,), (0,)), ((), ())), preferred_element_type=f32).astype(bf16)
        for q in range(4):
            mat_ref[pl.ds(pl.multiple_of(128 * spot + 16 * (chan ^ q), 16), 16), :] = turned[16 * q : 16 * q + 16]
        total = None
        for c in range(3):
            tap = 26 - 3 * spot - c
            block = jnp.concatenate([pack[16 * (tap % 8) : 16 * (tap % 8) + 16, 256:384] for pack in packs], axis=0)
            term = jnp.dot(block, picks[tap // 8, c], preferred_element_type=f32)
            total = term if total is None else total + term
        mat_ref[128 * spot + 64 : 128 * spot + 128] = total.astype(bf16)


def conv_layer(views, mat_ref):
    pieces = [view[80 * b : 80 * b + 640, :] for view in views for b in range(3)]
    sums = jnp.dot(jnp.concatenate(pieces, axis=1), mat_ref[...], preferred_element_type=f32).reshape(8, 80, 128)
    total = sums[:, 0:64] + pltpu.roll(sums[:, 8:72], 96, 2) + pltpu.roll(sums[:, 16:80], 64, 2)
    return total.reshape(512, 128)


def layers(grid_ref, mat_ref, done_ref, first, last):
    for x in range(first, last):
        views = [grid_ref.at[800 * (x + a - 1) : 800 * (x + a - 1) + 800] for a in range(3)]
        done_ref[512 * (x - first) : 512 * (x - first) + 512] = conv_layer(views, mat_ref)


def early_kernel(grid_ref, mat_ref, done_ref):
    layers(grid_ref, mat_ref, done_ref, 1, 1 + EARLY)


def late_kernel(grid_ref, mat_ref, done_ref):
    layers(grid_ref, mat_ref, done_ref, 1 + EARLY, 7)


def outer_kernel(near_ref, grid_ref, mat_ref, early_ref, late_ref, *refs):
    packs, (out, grad, planes, padded, edges, low, high, near, sem) = refs[:4], refs[4:]
    copy = pltpu.make_async_copy(near_ref, near, sem)
    copy.start()
    bricks = near_ref.shape[0]
    for s in range(bricks):
        rows = slice(16 * s, 16 * s + 16)
        pair = jnp.concatenate([pack[rows, 0:128] for pack in packs] + [pack[rows, 128:256] for pack in packs], axis=0)
        planes[128 * s : 128 * s + 128] = jnp.transpose(pair.astype(f32))
    planes[128 * bricks : 128 * bricks + 128] = jnp.zeros((128, 128), f32)
    copy.wait()
    pad_bricks(near, padded, planes, 128, [(0, 0, [(0, 0)]), (2, 64, [(1, 0)])])
    edges[...] = padded[...].astype(bf16)
    layers = [edges.at[0:800]] + [grid_ref.at[800 * x : 800 * x + 800] for x in (0, 1, 6, 7)] + [edges.at[800:1600]]
    low[...] = conv_layer(layers[0:3], mat_ref)
    high[...] = conv_layer(layers[3:6], mat_ref)
    for r in range(bricks):
        views = [view[pl.ds(r, view.shape[0] // 8, 8), :] for view in (low, early_ref, late_ref, high)]
        turned = jnp.transpose(jnp.concatenate(views, axis=0))
        out[r] = turned[0:16].astype(bf16)
        grad[r] = turned[16:32].astype(bf16)


def finish_kernel(out_ref, grad_ref, one_ref, other_ref, out_any, grad_any, kernel_any, kernel_grad, sems):
    copies = [
        pltpu.make_async_copy(out_ref, out_any, sems.at[0]),
        pltpu.make_async_copy(grad_ref, grad_any, sems.at[1]),
        pltpu.make_async_copy(kernel_grad, kernel_any, sems.at[2]),
    ]
    for copy in copies[:2]:
        copy.start()
    total = one_ref[...] + other_ref[...]
    for tap in range(27):
        for begin in (0, 8):
            row = 16 * tap + begin
            block = total[row % 216 : row % 216 + 8]
            kernel_grad[tap, begin : begin + 8] = block[:, 0:64] if row < 216 else block[:, 64:128]
    copies[2].start()
    for copy in copies:
        copy.wait()


def body(features, weight, cotangent, neighbours):
    bricks, narrow = features.shape[0], features.shape[1]
    rows = bricks * narrow
    length = lax.axis_size("space")
    shape = jax.ShapeDtypeStruct

    def across(name, value, apart, axis="chan"):
        with jax.named_scope(name):
            return lax.ppermute(value, axis, [(i, i ^ apart) for i in range(lax.axis_size(axis))])

    inputs = (features, cotangent, weight, neighbours)
    inputs = (features, cotangent, weight, neighbours)
    both, own, near, first, second = call(
        prepare_kernel,
        (
            shape((bricks, narrow, 1024), bf16),
            shape(weight.shape, bf16),
            shape(neighbours.shape, i32),
            shape((rows, 128), bf16),
            shape((rows, 128), bf16),
        ),
        [pltpu.SemaphoreType.DMA((4,))],
        *(pltpu.with_memory_space_constraint(view, pltpu.HBM) for view in inputs),
        specs=[HBM] * 4,
    )
    def meet(value, begin):
        mates = {i: i + 1 for i in range(begin, length - 1, 2)}
        mates.update({after: before for before, after in mates.items()})
        wide = lax.axis_size("chan")
        place = lambda i, c: mates[i] * wide + c if i in mates else i * wide + (c ^ 1)
        pairs = [(i * wide + c, place(i, c)) for i in range(length) for c in range(wide)]
        return lax.ppermute(value, ("space", "chan"), pairs)

    with jax.named_scope("plane_second"):
        second = meet(second, 1)
    with jax.named_scope("plane_first"):
        first = meet(first, 0)
    both1 = across("both_core", both, 1)
    feat2 = across("feat_y", features, 2)
    cot2 = across("cot_y", cotangent, 2)
    windows, sums = call(
        near_grad_kernel,
        (shape((14, 512, 256), bf16), shape((4, 32, 128), f32)),
        [pltpu.VMEM((3, 10, 10, 8, 128), f32), pltpu.VMEM((28, 2 * rows, 128), f32)],
        near, both, both1,
        specs=[VMEM] * 3,
    )
    second, first, sums = lax.optimization_barrier((second, first, sums))
    near_pack, far_pack = call(
        pack_kernel,
        (shape((rows, 384), bf16), shape((rows, 384), bf16)),
        [],
        second, first, own,
        specs=[VMEM] * 3,
    )
    feat2, windows = lax.optimization_barrier((feat2, windows))
    feat3 = across("feat_far", feat2, 1)
    edge_windows, sums = call(
        halo_grad_kernel,
        (shape((2, 64, 1152), bf16), shape((4, 32, 128), f32)),
        [pltpu.VMEM((2, 3, 10, 8, 128), f32), pltpu.VMEM((27, 2 * rows, 128), f32)],
        near, near_pack, both, both1, sums,
        specs=[VMEM] * 5,
    )
    part = call(
        functools.partial(far_grad_kernel, float(bricks * length * 512) ** -0.5),
        shape((216, 128), f32),
        [pltpu.VMEM((28, 2 * rows, 128), f32), pltpu.VMEM((4, 64, 128), f32)],
        windows, edge_windows, feat2, feat3, sums,
        specs=[VMEM] * 5,
    )
    steps = []
    step = 1
    while step < length:
        steps.append(step)
        step *= 2
    other = across("sum_first", part, steps[0], "space")
    cot2, far_pack, part = lax.optimization_barrier((cot2, far_pack, part))
    cot3 = across("cot_far", cot2, 1)
    far_pack2 = across("pack_y", far_pack, 2)
    near_pack1 = across("pack_core", near_pack, 1)
    far_pack3 = across("pack_far", far_pack2, 1)
    grid = call(
        inner_kernel,
        shape((6400, 128), bf16),
        [
            pltpu.VMEM(((bricks + 1) * 512, 128), f32),
            pltpu.VMEM((6400, 128), f32),
            pltpu.SMEM(neighbours.shape, i32),
            pltpu.SemaphoreType.DMA,
        ],
        near, both, both1, feat2, feat3, cot2, cot3,
        specs=[VMEM] * 7,
    )
    other, grid = lax.optimization_barrier((other, grid))
    matrix = call(
        matrix_kernel,
        shape((1152, 128), bf16),
        [],
        own, near_pack, near_pack1, far_pack2, far_pack3,
        specs=[VMEM] * 5,
    )
    early = call(early_kernel, shape((512 * EARLY, 128), f32), [], grid, matrix, specs=[VMEM, VMEM])
    for step in steps[1:]:
        part = part + other
        if step < steps[-1]:
            other = across("sum_next", part, step, "space")
            other, early, grid = lax.optimization_barrier((other, early, grid))
        else:
            other = across("sum_last", part, step, "space")
    late = call(late_kernel, shape((512 * (6 - EARLY), 128), f32), [], grid, matrix, specs=[VMEM, VMEM])
    output, grad_input = call(
        outer_kernel,
        (shape(features.shape, bf16), shape(features.shape, bf16)),
        [
            pltpu.VMEM(((bricks + 1) * 128, 128), f32),
            pltpu.VMEM((1600, 128), f32),
            pltpu.VMEM((1600, 128), bf16),
            pltpu.VMEM((512, 128), f32),
            pltpu.VMEM((512, 128), f32),
            pltpu.SMEM(neighbours.shape, i32),
            pltpu.SemaphoreType.DMA,
        ],
        near, grid, matrix, early, late, near_pack, near_pack1, far_pack2, far_pack3,
        specs=[VMEM] * 9,
    )
    return call(
        finish_kernel,
        (shape(features.shape, bf16), shape(features.shape, bf16), shape(weight.shape, f32)),
        [pltpu.VMEM(weight.shape, f32), pltpu.SemaphoreType.DMA((3,))],
        output, grad_input, part, other,
        specs=[VMEM] * 4,
        out_spec=HBM,
    )


def solution(mesh):
    in_specs = (
        P("space", "chan", None),
        P(None, "chan", None),
        P("space", "chan", None),
        P("space", None),
    )
    out_specs = (P("space", "chan", None), P("space", "chan", None), P(None, "chan", None))
    return jax.shard_map(body, mesh=mesh, in_specs=in_specs, out_specs=out_specs, check_vma=False)
```

```python
import functools

import jax
import jax.numpy as jnp
from jax import lax
from jax.experimental import pallas as pl
from jax.experimental.pallas import tpu as pltpu
from jax.sharding import PartitionSpec as P

f32, bf16, i32 = jnp.float32, jnp.bfloat16, jnp.int32
VMEM = pl.BlockSpec(memory_space=pltpu.VMEM)
HBM = pl.BlockSpec(memory_space=pltpu.HBM)

COSTS = {"pack_kernel": 2_000_000_000}
EARLY = 1
GROUPS = ((0, 8), (8, 14), (14, 22), (22, 27))


def iota(shape, axis):
    return lax.broadcasted_iota(i32, shape, axis)


def call(kernel, out_shape, scratch, *args, specs, out_spec=VMEM):
    name = getattr(kernel, "func", kernel).__name__
    return pl.pallas_call(
        kernel,
        name=name,
        out_shape=out_shape,
        in_specs=specs,
        out_specs=jax.tree.map(lambda _: out_spec, out_shape),
        scratch_shapes=scratch,
        compiler_params=pltpu.CompilerParams(vmem_limit_bytes=48 << 20),
        cost_estimate=pl.CostEstimate(flops=COSTS.get(name, 0), bytes_accessed=0, transcendentals=0),
    )(*args)


def prepare_kernel(feat_any, cot_any, weight_any, near_any, both_ref, weight_ref, near_ref, first_ref, second_ref, sems):
    rows = first_ref.shape[0]
    pairs = (
        (feat_any, both_ref.at[:, :, 0:512]),
        (cot_any, both_ref.at[:, :, 512:1024]),
        (weight_any, weight_ref),
        (near_any, near_ref),
    )
    copies = [pltpu.make_async_copy(source, target, sems.at[i]) for i, (source, target) in enumerate(pairs)]
    for copy in copies:
        copy.start()
    for copy in copies[:2]:
        copy.wait()
    low = jnp.concatenate([both_ref[:, :, i : i + 64].reshape(rows, 64) for i in (0, 512)], axis=1)
    high = jnp.concatenate([both_ref[:, :, i : i + 64].reshape(rows, 64) for i in (448, 960)], axis=1)
    even = lax.axis_index("space") % 2 == 0

    @pl.when(even)
    def _():
        first_ref[...] = high
        second_ref[...] = low

    @pl.when(jnp.logical_not(even))
    def _():
        first_ref[...] = low
        second_ref[...] = high

    for copy in copies[2:]:
        copy.wait()


def pack_kernel(second_ref, first_ref, weight_ref, near_pack_ref, far_pack_ref):
    rows = first_ref.shape[0]
    even = jnp.full((rows, 128), lax.axis_index("space") % 2, i32) == 0
    first, second = first_ref[...].astype(f32), second_ref[...].astype(f32)
    before = jnp.where(even, second, first)
    after = jnp.where(even, first, second)
    left = iota((rows, 128), 1) < 64
    feat = jnp.where(left, before, pltpu.roll(after, 64, 1)).astype(bf16)
    cot = jnp.where(left, pltpu.roll(before, 64, 1), after).astype(bf16)
    groups = []
    for group in range(4):
        taps = [weight_ref[8 * group + t] if 8 * group + t < 27 else jnp.zeros((16, 64), bf16) for t in range(8)]
        groups.append(jnp.concatenate(taps, axis=0))
    kernel = jnp.concatenate(groups, axis=1)
    spots, lanes = iota((256, 128), 0), iota((256, 128), 1)
    place = lax.axis_index("chan") // 2
    for target, pair in ((near_pack_ref, place), (far_pack_ref, place ^ 1)):
        target[:, 0:128] = feat
        target[:, 128:256] = cot
        owned = spots == 64 * (lanes // 32) + 32 * pair + lanes % 32
        part = jnp.dot(kernel, owned.astype(f32).astype(bf16), preferred_element_type=f32)
        target[:, 256:384] = part.astype(bf16)


def tap_sums(products, count, bricks, absent=()):
    lane_group = iota((16, 128), 1) // 16
    sums = []
    for begin, end in GROUPS:
        blocks = []
        for view in range(count):
            total = None
            for shift in range(8):
                chosen = None
                for brick in range(bricks):
                    start = (view * bricks + brick) * 16
                    tap = min(begin + (brick + shift) % 8, end - 1)
                    block = jnp.zeros((16, 128), f32) if tap in absent else products[tap, start : start + 16, :]
                    chosen = block if chosen is None else jnp.where(lane_group == brick, block, chosen)
                if shift:
                    chosen = pltpu.roll(chosen, 16 * shift, 1)
                total = chosen if total is None else total + chosen
            blocks.append(total)
        sums.append(blocks)
    return sums


def brick_picker(near_ref, rows):
    bricks = near_ref.shape[0]
    listed = near_ref[...]
    listed = jnp.where(listed < 0, bricks, listed % bricks).astype(f32)
    widen = (iota((bricks, rows), 1) // 16 == iota((bricks, rows), 0)).astype(f32)
    source = lax.dot_general(listed, widen, (((0,), (0,)), ((), ())), preferred_element_type=f32)
    source = source.astype(i32) * 16 + iota((27, rows), 1) % 16
    row_ids = iota((rows, rows), 0)

    def pick(i, j):
        first = 9 * i + 3 * j
        picks = [(row_ids == source[first + k : first + k + 1, :]).astype(f32).astype(bf16) for k in range(3)]
        return jnp.concatenate(picks, axis=1)

    return pick


def shifted_columns(columns, pick, j):
    if j != 1:
        columns = columns[:, 7:8] if j == 0 else columns[:, 0:1]
    wide, deep = columns.shape[0], columns.shape[1]
    count = wide * deep
    edge = iota((1, 8, 128), 1)
    moved = jnp.dot(columns.reshape(count * 8, 128), pick, preferred_element_type=f32)
    lower, own, upper = (moved[:, 128 * k : 128 * k + 128].reshape(count, 8, 128) for k in range(3))
    down = jnp.where(edge == 0, pltpu.roll(lower, 1, 1), pltpu.roll(own, 1, 1))
    up = jnp.where(edge == 7, pltpu.roll(upper, 7, 1), pltpu.roll(own, 7, 1))
    return [value.reshape(wide, deep, 8, 128) for value in (down, own, up)]


ROWS_TO = ((0, 1), (1, 9), (9, 10))


def near_grad_kernel(near_ref, both_ref, both1_ref, windows_ref, sums_ref, padded, products):
    bricks = near_ref.shape[0]
    rows = bricks * 16
    flat = jnp.transpose(both_ref[:, :, 512:1024].reshape(rows, 512).astype(f32)).astype(bf16).reshape(8, 8, 8, 128)
    pick = brick_picker(near_ref, rows)
    for x in (0, 9):
        padded[:, x] = jnp.zeros((3, 10, 8, 128), f32)
    for j in range(3):
        for c, value in enumerate(shifted_columns(flat, pick(1, j), j)):
            padded[c, 1:9, ROWS_TO[j][0] : ROWS_TO[j][1]] = value
    feat = jnp.concatenate([view[:, :, 0:512].reshape(rows, 512) for view in (both_ref, both1_ref)], axis=0)
    for pair in range(14):
        views = []
        for tap in (2 * pair, min(2 * pair + 1, 26)):
            a, b, c = (26 - tap) // 9, (26 - tap) // 3 % 3, (26 - tap) % 3
            views.append(padded[c, a : a + 8, b : b + 8].reshape(512, 128).astype(bf16))
        window = jnp.concatenate(views, axis=1)
        windows_ref[pair] = window
        both = jnp.dot(feat, window, preferred_element_type=f32)
        products[2 * pair] = both[:, 0:128]
        products[2 * pair + 1] = both[:, 128:256]
    sums = tap_sums(products, 2, bricks)
    for group in range(4):
        sums_ref[group] = jnp.concatenate(sums[group], axis=0)


def plane_ends(views, side):
    rows = views[0].shape[0] * 16
    start = 0 if side == 0 else 448
    return jnp.concatenate([view[:, :, start : start + 64].reshape(rows, 64) for view in views], axis=0)


def halo_grad_kernel(near_ref, packed_ref, both_ref, both1_ref, sums_ref, windows_ref, total_ref, edges, products):
    bricks = near_ref.shape[0]
    rows = bricks * 16
    planes = jnp.transpose(packed_ref[:, 128:256].astype(f32)).astype(bf16)
    pick = brick_picker(near_ref, rows)
    for side in range(2):
        columns = planes[64 * side : 64 * side + 64].reshape(1, 8, 8, 128)
        for j in range(3):
            for c, value in enumerate(shifted_columns(columns, pick(2 * side, j), j)):
                edges[side, c, ROWS_TO[j][0] : ROWS_TO[j][1]] = value.reshape(value.shape[1:])
    for side in range(2):
        views = []
        for place in range(9):
            b, c = (8 - place) // 3, (8 - place) % 3
            views.append(edges[side, c, b : b + 8].reshape(64, 128).astype(bf16))
        window = jnp.concatenate(views, axis=1)
        windows_ref[side] = window
        both = jnp.dot(plane_ends([both_ref, both1_ref], side), window, preferred_element_type=f32)
        for place in range(9):
            products[18 * (1 - side) + place] = both[:, 128 * place : 128 * place + 128]
    sums = tap_sums(products, 2, bricks, range(9, 18))
    for group in range(4):
        total_ref[group] = sums_ref[group] + jnp.concatenate(sums[group], axis=0)


def far_grad_kernel(scale, windows_ref, edge_windows_ref, feat2_ref, feat3_ref, sums_ref, part_ref, products, ordered):
    chan = lax.axis_index("chan")
    bricks = feat2_ref.shape[0]
    rows = bricks * 16
    far = jnp.concatenate([view[...].reshape(rows, 512) for view in (feat2_ref, feat3_ref)], axis=0)
    for pair in range(14):
        halves = []
        for index, tap in enumerate((2 * pair, min(2 * pair + 1, 26))):
            half = windows_ref[pair, :, 128 * index : 128 * index + 128]
            edge = slice(128 * (tap % 9), 128 * (tap % 9) + 128)
            if tap < 9:
                half = jnp.concatenate([half[0:448], edge_windows_ref[1, :, edge]], axis=0)
            elif tap >= 18:
                half = jnp.concatenate([edge_windows_ref[0, :, edge], half[64:512]], axis=0)
            halves.append(half)
        both = jnp.dot(far, jnp.concatenate(halves, axis=1), preferred_element_type=f32)
        products[2 * pair] = both[:, 0:128]
        products[2 * pair + 1] = both[:, 128:256]
    sums = tap_sums(products, 2, bricks)
    for group in range(4):
        both = sums_ref[group]
        for apart, block in enumerate((both[0:16], both[16:32], *sums[group])):
            ordered[group, pl.ds(pl.multiple_of(16 * (chan ^ apart), 16), 16), :] = block
    turned = [jnp.transpose(jnp.concatenate([ordered[i], ordered[i + 2]], axis=0)) * scale for i in range(2)]
    turned = jnp.concatenate([turned[0], turned[1][0:96]], axis=0)
    upper = jnp.concatenate([pltpu.roll(turned[216:224], 64, 1), turned[0:208]], axis=0)
    part_ref[...] = jnp.where(iota((216, 128), 1) < 64, turned[0:216], upper)


def pad_bricks(near, padded, source, size, xs):
    bricks = near.shape[0]
    for r in range(bricks):
        for i, base, x_pairs in xs:
            for j in range(3):
                for k in range(3):
                    listed = near[r, 9 * i + 3 * j + k]
                    start = jnp.where(listed < 0, bricks, listed % bricks) * size + base
                    y_pairs = [(y + 1, y) for y in range(8)] if j == 1 else [(0, 7) if j == 0 else (9, 0)]
                    z_to, z_from = (1, 0) if k == 1 else ((0, 7) if k == 0 else (9, 0))
                    if k == 1:
                        for x_to, x_from in x_pairs:
                            for y_to, y_from in y_pairs:
                                piece = source[pl.ds(start + 64 * x_from + 8 * y_from, 8), :]
                                padded[pl.ds(80 * (10 * x_to + y_to) + 8 + r, 8, 8), :] = piece
                    elif j == 1:
                        for x_to, x_from in x_pairs:
                            piece = source[pl.ds(start + 64 * x_from + z_from, 8, 8), :]
                            padded[pl.ds(80 * (10 * x_to + 1) + 8 * z_to + r, 8, 80), :] = piece
                    elif i == 1:
                        piece = source[pl.ds(start + 8 * y_pairs[0][1] + z_from, 8, 64), :]
                        padded[pl.ds(80 * y_pairs[0][0] + 8 * z_to + r, 8, 800), :] = piece
                    else:
                        piece = source[pl.ds(start + 8 * y_pairs[0][1] + z_from, 1), :]
                        padded[pl.ds(80 * (10 * x_pairs[0][0] + y_pairs[0][0]) + 8 * z_to + r, 1), :] = piece


def inner_kernel(near_ref, *refs):
    (both, both1), feats, cots, (grid_ref, flat, padded, near, sem) = refs[:2], refs[2:4], refs[4:6], refs[6:]
    copy = pltpu.make_async_copy(near_ref, near, sem)
    copy.start()
    bricks = near_ref.shape[0]
    feats = [both.at[:, :, 0:512], both1.at[:, :, 0:512], *feats]
    cots = [both.at[:, :, 512:1024], both1.at[:, :, 512:1024], *cots]
    for s in range(bricks):
        pair = jnp.concatenate([view[s] for view in feats + cots], axis=0)
        flat[512 * s : 512 * s + 512] = jnp.transpose(pair.astype(f32))
    flat[512 * bricks : 512 * bricks + 512] = jnp.zeros((512, 128), f32)
    copy.wait()
    pad_bricks(near, padded, flat, 512, [(1, 0, [(x, x) for x in range(8)])])
    for x in range(8):
        grid_ref[800 * x : 800 * x + 800] = padded[800 * x : 800 * x + 800].astype(bf16)


def matrix_kernel(weight_ref, *refs):
    packs, mat_ref = refs[:4], refs[4]
    chan = lax.axis_index("chan")
    lanes = iota((48, 128), 1)
    spots = iota((48, 128), 0)
    forward = (lanes == 32 * (spots // 16) + spots % 16).astype(f32).astype(bf16)
    lanes = iota((128, 128), 1)
    spots = iota((128, 128), 0)
    picks = {}
    for group in range(4):
        for c in range(3):
            hit = lanes - 32 * c - 16 == spots - 32 * group - 16 * (chan % 2)
            hit = hit & (lanes >= 32 * c + 16) & (lanes < 32 * c + 32)
            picks[group, c] = hit.astype(f32).astype(bf16)
    for spot in range(9):
        own = weight_ref[3 * spot : 3 * spot + 3].reshape(48, 64)
        turned = lax.dot_general(own, forward, (((0,), (0,)), ((), ())), preferred_element_type=f32).astype(bf16)
        for q in range(4):
            mat_ref[pl.ds(pl.multiple_of(128 * spot + 16 * (chan ^ q), 16), 16), :] = turned[16 * q : 16 * q + 16]
        total = None
        for c in range(3):
            tap = 26 - 3 * spot - c
            block = jnp.concatenate([pack[16 * (tap % 8) : 16 * (tap % 8) + 16, 256:384] for pack in packs], axis=0)
            term = jnp.dot(block, picks[tap // 8, c], preferred_element_type=f32)
            total = term if total is None else total + term
        mat_ref[128 * spot + 64 : 128 * spot + 128] = total.astype(bf16)


def conv_layer(views, mat_ref):
    pieces = [view[80 * b : 80 * b + 640, :] for view in views for b in range(3)]
    sums = jnp.dot(jnp.concatenate(pieces, axis=1), mat_ref[...], preferred_element_type=f32).reshape(8, 80, 128)
    total = sums[:, 0:64] + pltpu.roll(sums[:, 8:72], 96, 2) + pltpu.roll(sums[:, 16:80], 64, 2)
    return total.reshape(512, 128)


def layers(grid_ref, mat_ref, done_ref, first, last):
    for x in range(first, last):
        views = [grid_ref.at[800 * (x + a - 1) : 800 * (x + a - 1) + 800] for a in range(3)]
        done_ref[512 * (x - first) : 512 * (x - first) + 512] = conv_layer(views, mat_ref)


def early_kernel(grid_ref, mat_ref, done_ref):
    layers(grid_ref, mat_ref, done_ref, 1, 1 + EARLY)


def late_kernel(grid_ref, mat_ref, done_ref):
    layers(grid_ref, mat_ref, done_ref, 1 + EARLY, 7)


def outer_kernel(near_ref, grid_ref, mat_ref, early_ref, late_ref, *refs):
    packs, (out, grad, planes, padded, edges, low, high, near, sem) = refs[:4], refs[4:]
    copy = pltpu.make_async_copy(near_ref, near, sem)
    copy.start()
    bricks = near_ref.shape[0]
    for s in range(bricks):
        rows = slice(16 * s, 16 * s + 16)
        pair = jnp.concatenate([pack[rows, 0:128] for pack in packs] + [pack[rows, 128:256] for pack in packs], axis=0)
        planes[128 * s : 128 * s + 128] = jnp.transpose(pair.astype(f32))
    planes[128 * bricks : 128 * bricks + 128] = jnp.zeros((128, 128), f32)
    copy.wait()
    pad_bricks(near, padded, planes, 128, [(0, 0, [(0, 0)]), (2, 64, [(1, 0)])])
    edges[...] = padded[...].astype(bf16)
    layers = [edges.at[0:800]] + [grid_ref.at[800 * x : 800 * x + 800] for x in (0, 1, 6, 7)] + [edges.at[800:1600]]
    low[0:512] = conv_layer(layers[0:3], mat_ref)
    high[0:512] = conv_layer(layers[3:6], mat_ref)
    for r in range(bricks):
        views = [view[pl.ds(r, view.shape[0] // 8 - 1, 8), :] for view in (low, early_ref, late_ref, high)]
        turned = jnp.transpose(jnp.concatenate(views, axis=0))
        out[r] = turned[0:16].astype(bf16)
        grad[r] = turned[16:32].astype(bf16)


def finish_kernel(out_ref, grad_ref, one_ref, other_ref, out_any, grad_any, kernel_any, kernel_grad, sems):
    copies = [
        pltpu.make_async_copy(out_ref, out_any, sems.at[0]),
        pltpu.make_async_copy(grad_ref, grad_any, sems.at[1]),
        pltpu.make_async_copy(kernel_grad, kernel_any, sems.at[2]),
    ]
    for copy in copies[:2]:
        copy.start()
    total = one_ref[...] + other_ref[...]
    for tap in range(27):
        for begin in (0, 8):
            row = 16 * tap + begin
            block = total[row % 216 : row % 216 + 8]
            kernel_grad[tap, begin : begin + 8] = block[:, 0:64] if row < 216 else block[:, 64:128]
    copies[2].start()
    for copy in copies:
        copy.wait()


def body(features, weight, cotangent, neighbours):
    bricks, narrow = features.shape[0], features.shape[1]
    rows = bricks * narrow
    length = lax.axis_size("space")
    shape = jax.ShapeDtypeStruct

    def across(name, value, apart, axis="chan"):
        with jax.named_scope(name):
            return lax.ppermute(value, axis, [(i, i ^ apart) for i in range(lax.axis_size(axis))])

    inputs = (features, cotangent, weight, neighbours)
    inputs = (features, cotangent, weight, neighbours)
    both, own, near, first, second = call(
        prepare_kernel,
        (
            shape((bricks, narrow, 1024), bf16),
            shape(weight.shape, bf16),
            shape(neighbours.shape, i32),
            shape((rows, 128), bf16),
            shape((rows, 128), bf16),
        ),
        [pltpu.SemaphoreType.DMA((4,))],
        *(pltpu.with_memory_space_constraint(view, pltpu.HBM) for view in inputs),
        specs=[HBM] * 4,
    )
    def meet(value, begin):
        mates = {i: i + 1 for i in range(begin, length - 1, 2)}
        mates.update({after: before for before, after in mates.items()})
        wide = lax.axis_size("chan")
        place = lambda i, c: mates[i] * wide + c if i in mates else i * wide + (c ^ 1)
        pairs = [(i * wide + c, place(i, c)) for i in range(length) for c in range(wide)]
        return lax.ppermute(value, ("space", "chan"), pairs)

    with jax.named_scope("plane_second"):
        second = meet(second, 1)
    with jax.named_scope("plane_first"):
        first = meet(first, 0)
    both1 = across("both_core", both, 1)
    feat2 = across("feat_y", features, 2)
    cot2 = across("cot_y", cotangent, 2)
    windows, sums = call(
        near_grad_kernel,
        (shape((14, 512, 256), bf16), shape((4, 32, 128), f32)),
        [pltpu.VMEM((3, 10, 10, 8, 128), f32), pltpu.VMEM((28, 2 * rows, 128), f32)],
        near, both, both1,
        specs=[VMEM] * 3,
    )
    second, first, sums = lax.optimization_barrier((second, first, sums))
    near_pack, far_pack = call(
        pack_kernel,
        (shape((rows, 384), bf16), shape((rows, 384), bf16)),
        [],
        second, first, own,
        specs=[VMEM] * 3,
    )
    feat2, windows = lax.optimization_barrier((feat2, windows))
    feat3 = across("feat_far", feat2, 1)
    edge_windows, sums = call(
        halo_grad_kernel,
        (shape((2, 64, 1152), bf16), shape((4, 32, 128), f32)),
        [pltpu.VMEM((2, 3, 10, 8, 128), f32), pltpu.VMEM((27, 2 * rows, 128), f32)],
        near, near_pack, both, both1, sums,
        specs=[VMEM] * 5,
    )
    part = call(
        functools.partial(far_grad_kernel, float(bricks * length * 512) ** -0.5),
        shape((216, 128), f32),
        [pltpu.VMEM((28, 2 * rows, 128), f32), pltpu.VMEM((4, 64, 128), f32)],
        windows, edge_windows, feat2, feat3, sums,
        specs=[VMEM] * 5,
    )
    steps = []
    step = 1
    while step < length:
        steps.append(step)
        step *= 2
    other = across("sum_first", part, steps[0], "space")
    cot2, far_pack, part = lax.optimization_barrier((cot2, far_pack, part))
    cot3 = across("cot_far", cot2, 1)
    far_pack2 = across("pack_y", far_pack, 2)
    near_pack1 = across("pack_core", near_pack, 1)
    far_pack3 = across("pack_far", far_pack2, 1)
    grid = call(
        inner_kernel,
        shape((6400, 128), bf16),
        [
            pltpu.VMEM(((bricks + 1) * 512 + 64, 128), f32),
            pltpu.VMEM((7200, 128), f32),
            pltpu.SMEM(neighbours.shape, i32),
            pltpu.SemaphoreType.DMA,
        ],
        near, both, both1, feat2, feat3, cot2, cot3,
        specs=[VMEM] * 7,
    )
    other, grid = lax.optimization_barrier((other, grid))
    matrix = call(
        matrix_kernel,
        shape((1152, 128), bf16),
        [],
        own, near_pack, near_pack1, far_pack2, far_pack3,
        specs=[VMEM] * 5,
    )
    early = call(early_kernel, shape((512 * EARLY + 8, 128), f32), [], grid, matrix, specs=[VMEM, VMEM])
    for step in steps[1:]:
        part = part + other
        if step < steps[-1]:
            other = across("sum_next", part, step, "space")
            other, early, grid = lax.optimization_barrier((other, early, grid))
        else:
            other = across("sum_last", part, step, "space")
    late = call(late_kernel, shape((512 * (6 - EARLY) + 8, 128), f32), [], grid, matrix, specs=[VMEM, VMEM])
    output, grad_input = call(
        outer_kernel,
        (shape(features.shape, bf16), shape(features.shape, bf16)),
        [
            pltpu.VMEM(((bricks + 1) * 128 + 64, 128), f32),
            pltpu.VMEM((1600, 128), f32),
            pltpu.VMEM((1600, 128), bf16),
            pltpu.VMEM((520, 128), f32),
            pltpu.VMEM((520, 128), f32),
            pltpu.SMEM(neighbours.shape, i32),
            pltpu.SemaphoreType.DMA,
        ],
        near, grid, matrix, early, late, near_pack, near_pack1, far_pack2, far_pack3,
        specs=[VMEM] * 9,
    )
    return call(
        finish_kernel,
        (shape(features.shape, bf16), shape(features.shape, bf16), shape(weight.shape, f32)),
        [pltpu.VMEM(weight.shape, f32), pltpu.SemaphoreType.DMA((3,))],
        output, grad_input, part, other,
        specs=[VMEM] * 4,
        out_spec=HBM,
    )


def solution(mesh):
    in_specs = (
        P("space", "chan", None),
        P(None, "chan", None),
        P("space", "chan", None),
        P("space", None),
    )
    out_specs = (P("space", "chan", None), P("space", "chan", None), P(None, "chan", None))
    return jax.shard_map(body, mesh=mesh, in_specs=in_specs, out_specs=out_specs, check_vma=False)
```
